512 devices in a mesh: row: 64 (over z, x, core), chan: 8 (over y).
Axes of the slice: x: 4, y: 8, z: 8, core: 2. Of those that a mesh axis runs over, the one named last changes fastest.
Arguments:
- slide: bfloat16 [256, 512, 256], P('chan', 'row'), may hold values from -6 to 6
- kernel_taps: float32 [256, 31, 31], P('chan'), may hold values from -0.1875 to 0.1875
- w_in: bfloat16 [1024, 256], replicated, may hold values from -0.375 to 0.375
- w_out: bfloat16 [256, 1024], replicated, may hold values from -0.1875 to 0.1875
Outputs:
- block_out: bfloat16 [256, 512, 256], P('chan', 'row')
The draws below stay inside these ranges and needn't reach their ends.
All inputs are finite; a program needn't handle non-finite values.
Results may differ from the reference program's by a relative error of at most 0.0049.
Values may be sent and summed in bfloat16 or wider, within the bound.
A program may use at most 64 MiB of HBM per device.

```python
import jax
import jax.numpy as jnp
from jax import lax

C = 256
FF = 1024
KSIZE = 31
W = 256
H = 512


def levels(key, extent, split, smallest, largest):
    gain = 1.0
    for position, blocks in split:
        draws = jax.random.uniform(jax.random.fold_in(jax.random.fold_in(key, 6), position), (blocks,), jnp.float32, smallest / len(split), largest / len(split))
        gain = gain * jnp.repeat(jnp.exp(draws), extent[position] // blocks).reshape((-1,) + (1,) * (len(extent) - 1 - position))
    return gain


def gaussian(key, extent, deviation, limit, pieces=(), kind=jnp.bfloat16):
    array = deviation * jax.random.normal(key, extent, jnp.float32)
    if pieces:
        array = array * levels(key, extent, pieces, -0.22, 0.18)
    return jnp.clip(array, -limit, limit).astype(kind)


def setup_inputs(seed: int = 0) -> dict:
    splits = jax.random.split(jax.random.key(seed), 5)
    slide = gaussian(splits[0], (C, H, W), 1.0, 6.0, ((0, 8), (1, 64)))
    kernel_taps = gaussian(splits[1], (C, KSIZE, KSIZE), (KSIZE * KSIZE) ** -0.5, 0.1875, ((0, 8),), jnp.float32)
    w_in = gaussian(splits[2], (FF, C), C ** -0.5, 0.375)
    w_out = gaussian(splits[3], (C, FF), FF ** -0.5, 0.1875)
    return {"slide": slide, "kernel_taps": kernel_taps, "w_in": w_in, "w_out": w_out}


def channel_corr(pair):
    plane, taps = pair
    reach = (taps.shape[0] - 1) // 2
    padded = jnp.zeros((H, W), jnp.float32).at[: taps.shape[0], : taps.shape[1]].set(taps[::-1, ::-1])
    padded = jnp.roll(padded, (-reach, -reach), (0, 1))
    product = jnp.fft.fft2(plane) * jnp.fft.fft2(padded)
    return jnp.real(jnp.fft.ifft2(product)).astype(jnp.float32)


def reference(slide, kernel_taps, w_in, w_out):
    planes = slide.astype(jnp.float32)
    spatial = lax.map(channel_corr, (planes, kernel_taps))
    mixed = planes + spatial
    inner = mixed.astype(jnp.bfloat16)

    def row_mlp(pair):
        inner_row, mixed_row = pair
        hidden = jax.nn.gelu(jnp.dot(w_in, inner_row, preferred_element_type=jnp.float32), approximate=False).astype(jnp.bfloat16)
        branch = jnp.dot(w_out, hidden, preferred_element_type=jnp.float32).astype(jnp.bfloat16)
        return (mixed_row + branch.astype(jnp.float32)).astype(jnp.bfloat16)

    result = lax.map(row_mlp, (jnp.transpose(inner, (1, 0, 2)), jnp.transpose(mixed, (1, 0, 2))))
    return jnp.transpose(result, (1, 0, 2))
```

```python
import functools

import jax
import jax.numpy as jnp
from jax import lax
from jax.experimental import pallas as pl
from jax.experimental.pallas import tpu as pltpu
from jax.sharding import PartitionSpec as P

MESH = pl.DeviceIdType.MESH
F32 = jnp.float32
BF16 = jnp.bfloat16

TAPS = 31
STEP = 5
SPAN = 7
CH = 16
ROWS = 16
WIN = 48
GROUPS = 2
GCH = CH // GROUPS
PARTS = 4
PCH = CH // PARTS
HALVES = 2


def iota(shape, dim):
    return lax.broadcasted_iota(jnp.int32, shape, dim)


def kernel(
    chips,
    chans,
    slide,
    taps,
    w_in,
    w_out,
    out,
    xbuf,
    tbuf,
    toep,
    win_v,
    wout_v,
    mbuf,
    sbuf,
    rbuf,
    obuf,
    send1,
    recv1,
    send2,
    recv2,
    send3,
    recv3,
    loc,
):
    row = lax.axis_index("row")
    y = lax.axis_index("chan")
    chip = row // 2
    k = row % 2
    m = y * 2 + k
    peers = 2 * chans

    barrier = pltpu.get_barrier_semaphore()

    def greet(r, c):
        pl.semaphore_signal(barrier, inc=1, device_id=(r, c), device_id_type=MESH)

    for dq in (1, chips - 1):
        for tk in range(2):
            greet((chip + dq) % chips * 2 + tk, y)
    for d in range(1, peers):
        t = (m + d) % peers
        greet(chip * 2 + t % 2, t // 2)

    taps_copy = pltpu.make_async_copy(taps.at[pl.ds(k * CH, CH)], tbuf, loc.at[0])
    taps_copy.start()
    own_copy = pltpu.make_async_copy(slide.at[pl.ds(k * CH, CH)], xbuf.at[2 + k], loc.at[1])
    own_copy.start()
    win_copy = pltpu.make_async_copy(w_in, win_v, loc.at[2])
    win_copy.start()
    wout_copy = pltpu.make_async_copy(w_out, wout_v, loc.at[3])
    wout_copy.start()

    pl.semaphore_wait(barrier, 4 + peers - 1)

    halo = []
    for p in range(PARTS):
        for dq in (1, -1, 0):
            for tk in range(2) if dq else (None,):
                core = 1 - k if tk is None else tk
                first = core * CH + p * PCH
                copy = pltpu.make_async_remote_copy(
                    src_ref=slide.at[pl.ds(first, PCH)],
                    dst_ref=xbuf.at[(1 - dq) * 2 + k, pl.ds(p * PCH, PCH)],
                    send_sem=send1.at[p, 2 if tk is None else (1 - dq) * 2 + tk],
                    recv_sem=recv1.at[p, (1 - dq) * 2 + k],
                    device_id=((chip + dq + chips) % chips * 2 + core, y),
                    device_id_type=MESH,
                )
                copy.start()
                halo.append(copy)

    taps_copy.wait()
    lane = iota((TAPS, 256), 1)
    spread = (lane % WIN == iota((TAPS, 256), 0)) & (lane < STEP * WIN)
    spread = spread.astype(BF16)
    keep = lane // WIN == iota((TAPS, 256), 0) % STEP
    pick = (iota((SPAN * ROWS, TAPS), 0) // ROWS == iota((SPAN * ROWS, TAPS), 1) // STEP).astype(BF16)
    for c in range(CH):
        wide = lax.dot_general(
            tbuf[c].astype(BF16), spread, (((0,), (0,)), ((), ())), preferred_element_type=F32
        )
        wide = jnp.where(keep, wide, 0.0).astype(BF16)
        base = jnp.dot(pick, wide, preferred_element_type=F32)
        for b in range(SPAN):
            band = pltpu.roll(base[b * ROWS : (b + 1) * ROWS], 1, 1, stride=1, stride_axis=0)
            toep[c, pl.ds(b * ROWS, ROWS), :] = band.astype(BF16)

    own_copy.wait()
    zeros = jnp.zeros((256 - STEP * WIN, 256), BF16)
    exchange = []
    for g in range(GROUPS):
        for p in range(g * PARTS // GROUPS, (g + 1) * PARTS // GROUPS):
            for slot in (0, 1, 4, 5, 3 - k):
                part = xbuf.at[slot, pl.ds(p * PCH, PCH)]
                pltpu.make_async_copy(part, part, recv1.at[p, slot]).wait()
            for c in range(p * PCH, (p + 1) * PCH):
                x = jnp.concatenate([xbuf[j, c].astype(F32) for j in range(6)], axis=0)
                cols = [x.astype(BF16)]
                for b in range(1, STEP):
                    cols.append(pltpu.roll(x, 256 - b, 1).astype(BF16))
                prod = jnp.dot(toep[c], jnp.concatenate(cols + [zeros], axis=0), preferred_element_type=F32)
                total = x[ROWS : 2 * ROWS]
                for b in range(SPAN):
                    piece = prod[b * ROWS : (b + 1) * ROWS]
                    shift = (TAPS // 2 - STEP * b) % 256
                    total = total + (pltpu.roll(piece, shift, 1) if shift else piece)
                mbuf[c] = total
        mixed = mbuf[pl.ds(g * GCH, GCH)]
        sbuf[g] = jnp.swapaxes(mixed, 0, 1).astype(BF16)
        for d in range(1, peers):
            t = (m + d) % peers
            copy = pltpu.make_async_remote_copy(
                src_ref=sbuf.at[g, t % 2 * chans + t // 2],
                dst_ref=rbuf.at[g, m],
                send_sem=send2.at[g, d],
                recv_sem=recv2.at[g, m],
                device_id=(chip * 2 + t % 2, t // 2),
                device_id_type=MESH,
            )
            copy.start()
            exchange.append(copy)
        rbuf[g, m] = sbuf[g, k * chans + y]

    win_copy.wait()
    wout_copy.wait()
    for g in range(GROUPS):
        for d in range(1, peers):
            part = rbuf.at[g, (m + d) % peers]
            pltpu.make_async_copy(part, part, recv2.at[g, (m + d) % peers]).wait()
    wide = 256 // HALVES
    back = []
    for half in range(HALVES):
        px = pl.ds(half * wide, wide)
        inner = jnp.concatenate(
            [rbuf[g, s, :, px].astype(F32) for s in range(peers) for g in range(GROUPS)], axis=0
        )
        flat = inner.astype(BF16)
        branch = jnp.zeros((256, wide), F32)
        for f in range(4):
            v = jnp.dot(win_v[pl.ds(f * 256, 256), :], flat, preferred_element_type=F32)
            hidden = (v * (1.0 + lax.erf(v * (0.5**0.5))) * 0.5).astype(BF16)
            branch = branch + jnp.dot(wout_v[:, pl.ds(f * 256, 256)], hidden, preferred_element_type=F32)
        branch = branch.astype(BF16).astype(F32)
        obuf[half] = (inner + branch).astype(BF16)
        depth = 2 * CH
        for d in range(1, chans):
            t = (y + d) % chans
            copy = pltpu.make_async_remote_copy(
                src_ref=obuf.at[half, pl.ds(t * depth, depth)],
                dst_ref=out.at[half, y],
                send_sem=send3.at[half, d],
                recv_sem=recv3.at[half, y],
                device_id=(row, t),
                device_id_type=MESH,
            )
            copy.start()
            back.append(copy)
        out[half, y] = obuf[half, pl.ds(pl.multiple_of(y * depth, depth), depth), :]

    for copy in halo + exchange + back:
        copy.wait_send()
    for half in range(HALVES):
        for d in range(1, chans):
            part = out.at[half, (y + d) % chans]
            pltpu.make_async_copy(part, part, recv3.at[half, (y + d) % chans]).wait()


def solution(mesh):
    chips = mesh.shape["row"] // 2
    chans = mesh.shape["chan"]
    peers = 2 * chans
    placed = (P("chan", "row", None), P("chan", None, None), P(), P())

    def shards(slide, kernel_taps, w_in, w_out):
        depth, rows, width = slide.shape
        any_space = pl.BlockSpec(memory_space=pl.ANY)
        got = pl.pallas_call(
            functools.partial(kernel, chips, chans),
            out_shape=jax.ShapeDtypeStruct((HALVES, rows, depth, width // HALVES), BF16),
            in_specs=[any_space] * 4,
            out_specs=pl.BlockSpec(memory_space=pltpu.VMEM),
            scratch_shapes=[
                pltpu.VMEM((6, CH, rows, width), BF16),
                pltpu.VMEM((CH, TAPS, TAPS), F32),
                pltpu.VMEM((CH, SPAN * ROWS, 256), BF16),
                pltpu.VMEM(w_in.shape, BF16),
                pltpu.VMEM(w_out.shape, BF16),
                pltpu.VMEM((CH, ROWS, width), F32),
                pltpu.VMEM((GROUPS, ROWS, GCH, width), BF16),
                pltpu.VMEM((GROUPS, peers, GCH, width), BF16),
                pltpu.VMEM((HALVES, 256, width // HALVES), BF16),
                pltpu.SemaphoreType.DMA((PARTS, 6)),
                pltpu.SemaphoreType.DMA((PARTS, 6)),
                pltpu.SemaphoreType.DMA((GROUPS, peers)),
                pltpu.SemaphoreType.DMA((GROUPS, peers)),
                pltpu.SemaphoreType.DMA((HALVES, chans)),
                pltpu.SemaphoreType.DMA((HALVES, chans)),
                pltpu.SemaphoreType.DMA((4,)),
            ],
            compiler_params=pltpu.CompilerParams(
                collective_id=0, has_side_effects=True, vmem_limit_bytes=40 * 2**20
            ),
        )(slide, kernel_taps, w_in, w_out)
        return jnp.transpose(got, (2, 1, 0, 3)).reshape(slide.shape)

    return jax.shard_map(shards, mesh=mesh, in_specs=placed, out_specs=placed[0], check_vma=False)
```

```python
import functools

import jax
import jax.numpy as jnp
from jax import lax
from jax.experimental import pallas as pl
from jax.experimental.pallas import tpu as pltpu
from jax.sharding import PartitionSpec as P

MESH = pl.DeviceIdType.MESH
F32 = jnp.float32
BF16 = jnp.bfloat16

TAPS = 31
STEP = 5
SPAN = 7
CH = 16
ROWS = 16
WIN = 48
GROUPS = 2
GCH = CH // GROUPS
PARTS = 4
PCH = CH // PARTS


def iota(shape, dim):
    return lax.broadcasted_iota(jnp.int32, shape, dim)


def kernel(
    chips,
    chans,
    slide,
    taps,
    w_in,
    w_out,
    out,
    xbuf,
    tbuf,
    toep,
    win_v,
    wout_v,
    mbuf,
    sbuf,
    rbuf,
    obuf,
    send1,
    recv1,
    send2,
    recv2,
    send3,
    recv3,
    loc,
    ring2,
    ring4,
):
    row = lax.axis_index("row")
    y = lax.axis_index("chan")
    chip = row // 2
    k = row % 2
    m = y * 2 + k
    peers = 2 * chans
    last = chip == chips - 1

    barrier = pltpu.get_barrier_semaphore()

    def signal(sem, r, c):
        pl.semaphore_signal(sem, inc=1, device_id=(r, c), device_id_type=MESH)

    for dq in (1, chips - 1):
        for tk in range(2):
            signal(barrier, (chip + dq) % chips * 2 + tk, y)
    signal(barrier, chip * 2 + 1 - k, y)
    for dy in (1, chans - 1):
        for tk in range(2):
            signal(barrier, chip * 2 + tk, (y + dy) % chans)

    taps_copy = pltpu.make_async_copy(
        taps.at[:, pl.ds(pl.multiple_of(k * CH, CH), CH)], tbuf.at[pl.ds(0, TAPS)], loc.at[0]
    )
    own_copy = pltpu.make_async_copy(slide.at[pl.ds(k * CH, CH)], xbuf.at[2 + k], loc.at[1])
    win_copy = pltpu.make_async_copy(w_in, win_v, loc.at[2])
    wout_copy = pltpu.make_async_copy(w_out, wout_v, loc.at[3])
    for copy in (taps_copy, own_copy, win_copy, wout_copy):
        copy.start()

    def prepare():
        taps_copy.wait()
        tbuf[TAPS] = jnp.zeros(tbuf.shape[1:], F32)
        lane = iota((TAPS + 1, 256), 1)
        spread = (lane % WIN == iota((TAPS + 1, 256), 0)) & (lane < STEP * WIN)
        spread = spread.astype(BF16)
        keep = iota((TAPS, 256), 1) // WIN == iota((TAPS, 256), 0) % STEP
        pick = iota((SPAN * ROWS, TAPS), 0) // ROWS == iota((SPAN * ROWS, TAPS), 1) // STEP
        pick = pick.astype(BF16)
        plane = jnp.swapaxes(tbuf[...], 0, 1).astype(BF16)
        for c in range(CH):
            wide = lax.dot_general(plane[c], spread, (((0,), (0,)), ((), ())), preferred_element_type=F32)
            wide = jnp.where(keep, wide, 0.0).astype(BF16)
            base = jnp.dot(pick, wide, preferred_element_type=F32)
            for b in range(SPAN):
                band = pltpu.roll(base[b * ROWS : (b + 1) * ROWS], 1, 1, stride=1, stride_axis=0)
                toep[c, pl.ds(b * ROWS, ROWS), :] = band.astype(BF16)

    @pl.when(jnp.logical_not(last))
    def _():
        prepare()

    pl.semaphore_wait(barrier, 9)

    halo = []
    for dq in (1, -1, 0):
        for p in range(PARTS):
            for tk in range(2) if dq else (None,):
                core = 1 - k if tk is None else tk
                first = core * CH + p * PCH
                copy = pltpu.make_async_remote_copy(
                    src_ref=slide.at[pl.ds(first, PCH)],
                    dst_ref=xbuf.at[(1 - dq) * 2 + k, pl.ds(p * PCH, PCH)],
                    send_sem=send1.at[p, 2 if tk is None else (1 - dq) * 2 + tk],
                    recv_sem=recv1.at[p, (1 - dq) * 2 + k],
                    device_id=((chip + dq + chips) % chips * 2 + core, y),
                    device_id_type=MESH,
                )
                copy.start()
                halo.append(copy)

    @pl.when(last)
    def _():
        prepare()

    for dy in (1, chans - 1):
        signal(ring2, row, (y + dy) % chans)
    pl.semaphore_wait(ring2, 2)
    for dy in (2, chans - 2):
        signal(ring4, row, (y + dy) % chans)

    far = sorted(range(1, chans), key=lambda d: -min(d, chans - d))
    own_copy.wait()
    zeros = jnp.zeros((256 - STEP * WIN, 256), BF16)
    exchange = []
    for g in range(GROUPS):
        for p in range(g * PARTS // GROUPS, (g + 1) * PARTS // GROUPS):
            for slot in (0, 1, 4, 5, 3 - k):
                part = xbuf.at[slot, pl.ds(p * PCH, PCH)]
                pltpu.make_async_copy(part, part, recv1.at[p, slot]).wait()
            for c in range(p * PCH, (p + 1) * PCH):
                x = jnp.concatenate([xbuf[j, c].astype(F32) for j in range(6)], axis=0)
                cols = [x.astype(BF16)]
                for b in range(1, STEP):
                    cols.append(pltpu.roll(x, 256 - b, 1).astype(BF16))
                prod = jnp.dot(toep[c], jnp.concatenate(cols + [zeros], axis=0), preferred_element_type=F32)
                total = x[ROWS : 2 * ROWS]
                for b in range(SPAN):
                    piece = prod[b * ROWS : (b + 1) * ROWS]
                    shift = (TAPS // 2 - STEP * b) % 256
                    total = total + (pltpu.roll(piece, shift, 1) if shift else piece)
                mbuf[c] = total
        mixed = mbuf[pl.ds(g * GCH, GCH)]
        sbuf[g] = jnp.swapaxes(mixed, 0, 1).astype(BF16)
        if g == 0:
            pl.semaphore_wait(ring4, 2)
        for d in far + [0]:
            for tk in (0, 1) if d else (None,):
                core = 1 - k if tk is None else tk
                t = (y + d) % chans
                copy = pltpu.make_async_remote_copy(
                    src_ref=sbuf.at[g, core * chans + t],
                    dst_ref=rbuf.at[g, m],
                    send_sem=send2.at[g, 2 * d + (tk or 0)],
                    recv_sem=recv2.at[g, m],
                    device_id=(chip * 2 + core, t),
                    device_id_type=MESH,
                )
                copy.start()
                exchange.append(copy)
        rbuf[g, m] = sbuf[g, k * chans + y]

    win_copy.wait()
    wout_copy.wait()
    for g in range(GROUPS):
        for d in range(1, peers):
            part = rbuf.at[g, (m + d) % peers]
            pltpu.make_async_copy(part, part, recv2.at[g, (m + d) % peers]).wait()
    inner = jnp.concatenate([rbuf[g, s].astype(F32) for s in range(peers) for g in range(GROUPS)], axis=0)
    flat = inner.astype(BF16)
    branch = jnp.zeros((256, 256), F32)
    for f in range(4):
        v = jnp.dot(win_v[pl.ds(f * 256, 256), :], flat, preferred_element_type=F32)
        hidden = (v * (1.0 + lax.erf(v * (0.5**0.5))) * 0.5).astype(BF16)
        branch = branch + jnp.dot(wout_v[:, pl.ds(f * 256, 256)], hidden, preferred_element_type=F32)
    obuf[...] = (inner + branch.astype(BF16).astype(F32)).astype(BF16)
    back = []
    depth = 2 * CH
    for d in far:
        t = (y + d) % chans
        copy = pltpu.make_async_remote_copy(
            src_ref=obuf.at[pl.ds(pl.multiple_of(t * depth, depth), depth)],
            dst_ref=out.at[y],
            send_sem=send3.at[d],
            recv_sem=recv3.at[y],
            device_id=(row, t),
            device_id_type=MESH,
        )
        copy.start()
        back.append(copy)
    out[y] = obuf[pl.ds(pl.multiple_of(y * depth, depth), depth), :]

    for copy in halo + exchange + back:
        copy.wait_send()
    for d in range(1, chans):
        part = out.at[(y + d) % chans]
        pltpu.make_async_copy(part, part, recv3.at[(y + d) % chans]).wait()


def solution(mesh):
    chips = mesh.shape["row"] // 2
    chans = mesh.shape["chan"]
    peers = 2 * chans
    placed = (P("chan", "row", None), P("chan", None, None), P(), P())

    def shards(slide, kernel_taps, w_in, w_out):
        depth, rows, width = slide.shape
        hbm = pl.BlockSpec(memory_space=pltpu.HBM)
        got = pl.pallas_call(
            functools.partial(kernel, chips, chans),
            out_shape=jax.ShapeDtypeStruct((rows, depth, width), BF16),
            in_specs=[hbm] * 4,
            out_specs=pl.BlockSpec(memory_space=pltpu.VMEM),
            scratch_shapes=[
                pltpu.VMEM((6, CH, rows, width), BF16),
                pltpu.VMEM((TAPS + 1, CH, TAPS), F32),
                pltpu.VMEM((CH, SPAN * ROWS, 256), BF16),
                pltpu.VMEM(w_in.shape, BF16),
                pltpu.VMEM(w_out.shape, BF16),
                pltpu.VMEM((CH, ROWS, width), F32),
                pltpu.VMEM((GROUPS, ROWS, GCH, width), BF16),
                pltpu.VMEM((GROUPS, peers, GCH, width), BF16),
                pltpu.VMEM((256, width), BF16),
                pltpu.SemaphoreType.DMA((PARTS, 6)),
                pltpu.SemaphoreType.DMA((PARTS, 6)),
                pltpu.SemaphoreType.DMA((GROUPS, peers)),
                pltpu.SemaphoreType.DMA((GROUPS, peers)),
                pltpu.SemaphoreType.DMA((chans,)),
                pltpu.SemaphoreType.DMA((chans,)),
                pltpu.SemaphoreType.DMA((4,)),
                pltpu.SemaphoreType.REGULAR,
                pltpu.SemaphoreType.REGULAR,
            ],
            compiler_params=pltpu.CompilerParams(
                collective_id=0, has_side_effects=True, vmem_limit_bytes=60 * 2**20
            ),
        )(slide, jnp.transpose(kernel_taps, (1, 0, 2)), w_in, w_out)
        return jnp.transpose(got, (1, 0, 2))

    return jax.shard_map(shards, mesh=mesh, in_specs=placed, out_specs=placed[0], check_vma=False)
```

```python
import functools

import jax
import jax.numpy as jnp
from jax import lax
from jax.experimental import pallas as pl
from jax.experimental.pallas import tpu as pltpu
from jax.sharding import PartitionSpec as P

MESH = pl.DeviceIdType.MESH
F32 = jnp.float32
BF16 = jnp.bfloat16

TAPS = 31
STEP = 5
SPAN = 7
CH = 16
ROWS = 16
WIN = 48
GROUPS = 2
GCH = CH // GROUPS
PARTS = 4
PCH = CH // PARTS


def iota(shape, dim):
    return lax.broadcasted_iota(jnp.int32, shape, dim)


def kernel(
    chips,
    chans,
    slide,
    taps,
    w_in,
    w_out,
    out,
    xbuf,
    tbuf,
    toep,
    win_v,
    wout_v,
    mbuf,
    sbuf,
    rbuf,
    obuf,
    send1,
    recv1,
    send2,
    recv2,
    send3,
    recv3,
    loc,
    back_x,
):
    row = lax.axis_index("row")
    y = lax.axis_index("chan")
    chip = row // 2
    k = row % 2
    m = y * 2 + k
    peers = 2 * chans
    last = chip == chips - 1
    below = (chip + 1) % chips
    above = (chip + chips - 1) % chips

    def signal(sem, r, c):
        pl.semaphore_signal(sem, inc=1, device_id=(r, c), device_id_type=MESH)

    barrier = pltpu.get_barrier_semaphore()
    for tk in range(2):
        signal(barrier, above * 2 + tk, y)
    signal(barrier, chip * 2 + 1 - k, y)
    base = jnp.where(last, above, chip)
    for d in range(1, chans):
        for tk in range(2):
            signal(barrier, base * 2 + tk, (y + d) % chans)

    taps_copy = pltpu.make_async_copy(
        taps.at[:, pl.ds(pl.multiple_of(k * CH, CH), CH)], tbuf.at[pl.ds(0, TAPS)], loc.at[0]
    )
    own_copy = pltpu.make_async_copy(slide.at[pl.ds(k * CH, CH)], xbuf.at[2 + k], loc.at[1])
    win_copy = pltpu.make_async_copy(w_in, win_v, loc.at[2])
    wout_copy = pltpu.make_async_copy(w_out, wout_v, loc.at[3])
    for copy in (taps_copy, own_copy, win_copy, wout_copy):
        copy.start()

    def prepare():
        taps_copy.wait()
        tbuf[TAPS] = jnp.zeros(tbuf.shape[1:], F32)
        lane = iota((TAPS + 1, 256), 1)
        spread = (lane % WIN == iota((TAPS + 1, 256), 0)) & (lane < STEP * WIN)
        spread = spread.astype(BF16)
        keep = iota((TAPS, 256), 1) // WIN == iota((TAPS, 256), 0) % STEP
        pick = iota((SPAN * ROWS, TAPS), 0) // ROWS == iota((SPAN * ROWS, TAPS), 1) // STEP
        pick = pick.astype(BF16)
        plane = jnp.swapaxes(tbuf[...], 0, 1).astype(BF16)
        for c in range(CH):
            wide = lax.dot_general(plane[c], spread, (((0,), (0,)), ((), ())), preferred_element_type=F32)
            wide = jnp.where(keep, wide, 0.0).astype(BF16)
            base = jnp.dot(pick, wide, preferred_element_type=F32)
            for b in range(SPAN):
                band = pltpu.roll(base[b * ROWS : (b + 1) * ROWS], 1, 1, stride=1, stride_axis=0)
                toep[c, pl.ds(b * ROWS, ROWS), :] = band.astype(BF16)

    @pl.when(jnp.logical_not(last))
    def _():
        prepare()

    pl.semaphore_wait(barrier, jnp.where(last, 3, jnp.where(chip == chips - 2, 2 * peers - 1, peers + 1)))

    for tk in range(2):
        signal(back_x, below * 2 + tk, y)

    halo = []

    def send_rows(dq):
        for p in range(PARTS):
            for tk in range(2) if dq else (None,):
                core = 1 - k if tk is None else tk
                first = core * CH + p * PCH
                copy = pltpu.make_async_remote_copy(
                    src_ref=slide.at[pl.ds(first, PCH)],
                    dst_ref=xbuf.at[(1 - dq) * 2 + k, pl.ds(p * PCH, PCH)],
                    send_sem=send1.at[p, 2 if tk is None else (1 - dq) * 2 + tk],
                    recv_sem=recv1.at[p, (1 - dq) * 2 + k],
                    device_id=({1: below, 0: chip, -1: above}[dq] * 2 + core, y),
                    device_id_type=MESH,
                )
                copy.start()
                halo.append(copy)

    send_rows(1)
    send_rows(0)

    pl.semaphore_wait(back_x, 2)
    send_rows(-1)

    @pl.when(last)
    def _():
        prepare()

    far = sorted(range(1, chans), key=lambda d: -min(d, chans - d))
    own_copy.wait()
    zeros = jnp.zeros((256 - STEP * WIN, 256), BF16)
    exchange = []
    for g in range(GROUPS):
        for p in range(g * PARTS // GROUPS, (g + 1) * PARTS // GROUPS):
            for slot in (0, 1, 4, 5, 3 - k):
                part = xbuf.at[slot, pl.ds(p * PCH, PCH)]
                pltpu.make_async_copy(part, part, recv1.at[p, slot]).wait()
            for c in range(p * PCH, (p + 1) * PCH):
                x = jnp.concatenate([xbuf[j, c].astype(F32) for j in range(6)], axis=0)
                cols = [x.astype(BF16)]
                for b in range(1, STEP):
                    cols.append(pltpu.roll(cols[0], 256 - b, 1))
                prod = jnp.dot(toep[c], jnp.concatenate(cols + [zeros], axis=0), preferred_element_type=F32)
                total = x[ROWS : 2 * ROWS]
                for b in range(SPAN):
                    piece = prod[b * ROWS : (b + 1) * ROWS]
                    shift = (TAPS // 2 - STEP * b) % 256
                    total = total + (pltpu.roll(piece, shift, 1) if shift else piece)
                mbuf[c] = total
        mixed = mbuf[pl.ds(g * GCH, GCH)]
        sbuf[g] = jnp.swapaxes(mixed, 0, 1).astype(BF16)
        for d in far + [0]:
            for tk in (0, 1) if d else (None,):
                core = 1 - k if tk is None else tk
                t = (y + d) % chans
                copy = pltpu.make_async_remote_copy(
                    src_ref=sbuf.at[g, core * chans + t],
                    dst_ref=rbuf.at[g, m],
                    send_sem=send2.at[g, 2 * d + (tk or 0)],
                    recv_sem=recv2.at[g, m],
                    device_id=(chip * 2 + core, t),
                    device_id_type=MESH,
                )
                copy.start()
                exchange.append(copy)
        rbuf[g, m] = sbuf[g, k * chans + y]

    win_copy.wait()
    wout_copy.wait()
    for g in range(GROUPS):
        for d in range(1, peers):
            part = rbuf.at[g, (m + d) % peers]
            pltpu.make_async_copy(part, part, recv2.at[g, (m + d) % peers]).wait()
    inner = jnp.concatenate([rbuf[g, s].astype(F32) for s in range(peers) for g in range(GROUPS)], axis=0)
    flat = inner.astype(BF16)
    branch = jnp.zeros((256, 256), F32)
    for f in range(4):
        v = jnp.dot(win_v[pl.ds(f * 256, 256), :], flat, preferred_element_type=F32)
        hidden = (v * (1.0 + lax.erf(v * (0.5**0.5))) * 0.5).astype(BF16)
        branch = branch + jnp.dot(wout_v[:, pl.ds(f * 256, 256)], hidden, preferred_element_type=F32)
    result = (inner + branch.astype(BF16).astype(F32)).astype(BF16)
    obuf[0] = result[:, :128]
    obuf[1] = result[:, 128:]
    depth = 2 * CH
    targets = sorted(range(chans), key=lambda t: min(t, chans - t))
    back = []
    for t in targets:
        copy = pltpu.make_async_remote_copy(
            src_ref=obuf.at[:, pl.ds(t * depth, depth)],
            dst_ref=out.at[:, y],
            send_sem=send3.at[t],
            recv_sem=recv3.at[y],
            device_id=(row, t),
            device_id_type=MESH,
        )
        pl.when(y != t)(copy.start)
        back.append(copy)
    out[:, y] = obuf[:, pl.ds(pl.multiple_of(y * depth, depth), depth), :]

    for copy in halo + exchange:
        copy.wait_send()
    for t, copy in zip(targets, back):
        pl.when(y != t)(copy.wait_send)
    for d in range(1, chans):
        part = out.at[:, (y + d) % chans]
        pltpu.make_async_copy(part, part, recv3.at[(y + d) % chans]).wait()


def solution(mesh):
    chips = mesh.shape["row"] // 2
    chans = mesh.shape["chan"]
    peers = 2 * chans
    placed = (P("chan", "row", None), P("chan", None, None), P(), P())

    def shards(slide, kernel_taps, w_in, w_out):
        depth, rows, width = slide.shape
        hbm = pl.BlockSpec(memory_space=pltpu.HBM)
        got = pl.pallas_call(
            functools.partial(kernel, chips, chans),
            out_shape=jax.ShapeDtypeStruct((2, rows, depth, width // 2), BF16),
            in_specs=[hbm] * 4,
            out_specs=pl.BlockSpec(memory_space=pltpu.VMEM),
            scratch_shapes=[
                pltpu.VMEM((6, CH, rows, width), BF16),
                pltpu.VMEM((TAPS + 1, CH, TAPS), F32),
                pltpu.VMEM((CH, SPAN * ROWS, 256), BF16),
                pltpu.VMEM(w_in.shape, BF16),
                pltpu.VMEM(w_out.shape, BF16),
                pltpu.VMEM((CH, ROWS, width), F32),
                pltpu.VMEM((GROUPS, ROWS, GCH, width), BF16),
                pltpu.VMEM((GROUPS, peers, GCH, width), BF16),
                pltpu.VMEM((2, 256, width // 2), BF16),
                pltpu.SemaphoreType.DMA((PARTS, 6)),
                pltpu.SemaphoreType.DMA((PARTS, 6)),
                pltpu.SemaphoreType.DMA((GROUPS, peers)),
                pltpu.SemaphoreType.DMA((GROUPS, peers)),
                pltpu.SemaphoreType.DMA((chans,)),
                pltpu.SemaphoreType.DMA((chans,)),
                pltpu.SemaphoreType.DMA((4,)),
                pltpu.SemaphoreType.REGULAR,
            ],
            compiler_params=pltpu.CompilerParams(
                collective_id=0, has_side_effects=True, vmem_limit_bytes=60 * 2**20
            ),
        )(slide, jnp.transpose(kernel_taps, (1, 0, 2)), w_in, w_out)
        return jnp.transpose(got, (2, 1, 0, 3)).reshape(slide.shape)

    return jax.shard_map(shards, mesh=mesh, in_specs=placed, out_specs=placed[0], check_vma=False)
```

```python
import functools

import jax
import jax.numpy as jnp
from jax import lax
from jax.experimental import pallas as pl
from jax.experimental.pallas import tpu as pltpu
from jax.sharding import PartitionSpec as P

MESH = pl.DeviceIdType.MESH
F32 = jnp.float32
BF16 = jnp.bfloat16

TAPS = 31
STEP = 5
SPAN = 7
CH = 16
ROWS = 16
WIN = 48
GROUPS = 2
GCH = CH // GROUPS
PARTS = 4
PCH = CH // PARTS


def iota(shape, dim):
    return lax.broadcasted_iota(jnp.int32, shape, dim)


def kernel(
    chips,
    chans,
    slide,
    taps,
    w_in,
    w_out,
    out,
    xbuf,
    tbuf,
    toep,
    win_v,
    wout_v,
    mbuf,
    sbuf,
    rbuf,
    obuf,
    send1,
    recv1,
    send2,
    recv2,
    send3,
    recv3,
    loc,
    back_x,
):
    row = lax.axis_index("row")
    y = lax.axis_index("chan")
    chip = row // 2
    k = row % 2
    m = y * 2 + k
    peers = 2 * chans
    last = chip == chips - 1
    below = (chip + 1) % chips
    above = (chip + chips - 1) % chips

    def signal(sem, r, c):
        pl.semaphore_signal(sem, inc=1, device_id=(r, c), device_id_type=MESH)

    barrier = pltpu.get_barrier_semaphore()
    for tk in range(2):
        signal(barrier, above * 2 + tk, y)

    def row_copy(dq, p, tk):
        core = 1 - k if dq == 0 else tk
        first = core * CH + p * PCH
        return pltpu.make_async_remote_copy(
            src_ref=slide.at[pl.ds(first, PCH)],
            dst_ref=xbuf.at[(1 - dq) * 2 + k, pl.ds(p * PCH, PCH)],
            send_sem=send1.at[p, (1 - dq) * 2 + tk],
            recv_sem=recv1.at[p, (1 - dq) * 2 + k],
            device_id=({1: below, 0: chip, -1: above}[dq] * 2 + core, y),
            device_id_type=MESH,
        )

    def send_rows(dq):
        for p in range(PARTS):
            for tk in range(2 if dq else 1):
                row_copy(dq, p, tk).start()

    @pl.when(last)
    def _():
        pl.semaphore_wait(barrier, 2)
        send_rows(1)

    base = jnp.where(last, above, chip)
    for d in range(1, chans):
        for tk in range(2):
            signal(barrier, base * 2 + tk, (y + d) % chans)

    @pl.when(jnp.logical_not(last))
    def _():
        signal(barrier, chip * 2 + 1 - k, y)

    @pl.when(chip < chips - 2)
    def _():
        for tk in range(2):
            signal(barrier, below * 2 + tk, y)

    taps_copy = pltpu.make_async_copy(
        taps.at[:, pl.ds(pl.multiple_of(k * CH, CH), CH)], tbuf.at[pl.ds(0, TAPS)], loc.at[0]
    )
    own_copy = pltpu.make_async_copy(slide.at[pl.ds(k * CH, CH)], xbuf.at[2 + k], loc.at[1])
    win_copy = pltpu.make_async_copy(w_in, win_v, loc.at[2])
    wout_copy = pltpu.make_async_copy(w_out, wout_v, loc.at[3])
    for copy in (taps_copy, own_copy, win_copy, wout_copy):
        copy.start()

    def prepare():
        taps_copy.wait()
        tbuf[TAPS] = jnp.zeros(tbuf.shape[1:], F32)
        lane = iota((TAPS + 1, 256), 1)
        spread = (lane % WIN == iota((TAPS + 1, 256), 0)) & (lane < STEP * WIN)
        spread = spread.astype(BF16)
        keep = iota((TAPS, 256), 1) // WIN == iota((TAPS, 256), 0) % STEP
        pick = iota((SPAN * ROWS, TAPS), 0) // ROWS == iota((SPAN * ROWS, TAPS), 1) // STEP
        pick = pick.astype(BF16)
        plane = jnp.swapaxes(tbuf[...], 0, 1).astype(BF16)
        for c in range(CH):
            wide = lax.dot_general(plane[c], spread, (((0,), (0,)), ((), ())), preferred_element_type=F32)
            wide = jnp.where(keep, wide, 0.0).astype(BF16)
            base = jnp.dot(pick, wide, preferred_element_type=F32)
            for b in range(SPAN):
                band = pltpu.roll(base[b * ROWS : (b + 1) * ROWS], 1, 1, stride=1, stride_axis=0)
                toep[c, pl.ds(b * ROWS, ROWS), :] = band.astype(BF16)

    @pl.when(jnp.logical_not(last))
    def _():
        prepare()
        from_above = jnp.where(chip == 0, 0, 2)
        from_below = jnp.where(chip == chips - 2, peers, 2)
        pl.semaphore_wait(barrier, peers - 1 + from_above + from_below)
        send_rows(1)

    @pl.when(chip >= chips - 2)
    def _():
        for tk in range(2):
            signal(back_x, below * 2 + tk, y)

    @pl.when(jnp.logical_or(last, chip == 0))
    def _():
        pl.semaphore_wait(back_x, 2)

    send_rows(0)
    send_rows(-1)

    @pl.when(last)
    def _():
        prepare()

    far = sorted(range(1, chans), key=lambda d: -min(d, chans - d))
    own_copy.wait()
    zeros = jnp.zeros((256 - STEP * WIN, 256), BF16)
    exchange = []
    for g in range(GROUPS):
        for p in range(g * PARTS // GROUPS, (g + 1) * PARTS // GROUPS):
            for slot in (0, 1, 4, 5, 3 - k):
                part = xbuf.at[slot, pl.ds(p * PCH, PCH)]
                pltpu.make_async_copy(part, part, recv1.at[p, slot]).wait()
            for c in range(p * PCH, (p + 1) * PCH):
                x = jnp.concatenate([xbuf[j, c].astype(F32) for j in range(6)], axis=0)
                cols = [x.astype(BF16)]
                for b in range(1, STEP):
                    cols.append(pltpu.roll(cols[0], 256 - b, 1))
                prod = jnp.dot(toep[c], jnp.concatenate(cols + [zeros], axis=0), preferred_element_type=F32)
                total = x[ROWS : 2 * ROWS]
                for b in range(SPAN):
                    piece = prod[b * ROWS : (b + 1) * ROWS]
                    shift = (TAPS // 2 - STEP * b) % 256
                    total = total + (pltpu.roll(piece, shift, 1) if shift else piece)
                mbuf[c] = total
        mixed = mbuf[pl.ds(g * GCH, GCH)]
        sbuf[g] = jnp.swapaxes(mixed, 0, 1).astype(BF16)
        for d in far + [0]:
            for tk in (0, 1) if d else (None,):
                core = 1 - k if tk is None else tk
                t = (y + d) % chans
                copy = pltpu.make_async_remote_copy(
                    src_ref=sbuf.at[g, core * chans + t],
                    dst_ref=rbuf.at[g, m],
                    send_sem=send2.at[g, 2 * d + (tk or 0)],
                    recv_sem=recv2.at[g, m],
                    device_id=(chip * 2 + core, t),
                    device_id_type=MESH,
                )
                copy.start()
                exchange.append(copy)
        rbuf[g, m] = sbuf[g, k * chans + y]

    win_copy.wait()
    wout_copy.wait()
    for g in range(GROUPS):
        for d in range(1, peers):
            part = rbuf.at[g, (m + d) % peers]
            pltpu.make_async_copy(part, part, recv2.at[g, (m + d) % peers]).wait()
    inner = jnp.concatenate([rbuf[g, s].astype(F32) for s in range(peers) for g in range(GROUPS)], axis=0)
    flat = inner.astype(BF16)
    branch = jnp.zeros((256, 256), F32)
    for f in range(4):
        v = jnp.dot(win_v[pl.ds(f * 256, 256), :], flat, preferred_element_type=F32)
        hidden = (v * (1.0 + lax.erf(v * (0.5**0.5))) * 0.5).astype(BF16)
        branch = branch + jnp.dot(wout_v[:, pl.ds(f * 256, 256)], hidden, preferred_element_type=F32)
    result = (inner + branch.astype(BF16).astype(F32)).astype(BF16)
    obuf[0] = result[:, :128]
    obuf[1] = result[:, 128:]
    depth = 2 * CH

    def send_back(t, slot):
        return pltpu.make_async_remote_copy(
            src_ref=obuf.at[:, pl.ds(pl.multiple_of(t * depth, depth), depth)],
            dst_ref=out.at[:, y],
            send_sem=send3.at[slot],
            recv_sem=recv3.at[y],
            device_id=(row, t),
            device_id_type=MESH,
        )

    pl.when(y > 0)(send_back(0, 0).start)
    for d in far:
        t = (y + d) % chans
        pl.when(t > 0)(send_back(t, d).start)
    out[:, y] = obuf[:, pl.ds(pl.multiple_of(y * depth, depth), depth), :]

    for p in range(PARTS):
        for dq in (1, 0, -1):
            for tk in range(2 if dq else 1):
                row_copy(dq, p, tk).wait_send()
    for copy in exchange:
        copy.wait_send()
    pl.when(y > 0)(send_back(0, 0).wait_send)
    for d in far:
        t = (y + d) % chans
        pl.when(t > 0)(send_back(t, d).wait_send)
    for d in range(1, chans):
        part = out.at[:, (y + d) % chans]
        pltpu.make_async_copy(part, part, recv3.at[(y + d) % chans]).wait()


def solution(mesh):
    chips = mesh.shape["row"] // 2
    chans = mesh.shape["chan"]
    peers = 2 * chans
    placed = (P("chan", "row", None), P("chan", None, None), P(), P())

    def shards(slide, kernel_taps, w_in, w_out):
        depth, rows, width = slide.shape
        hbm = pl.BlockSpec(memory_space=pltpu.HBM)
        got = pl.pallas_call(
            functools.partial(kernel, chips, chans),
            out_shape=jax.ShapeDtypeStruct((2, rows, depth, width // 2), BF16),
            in_specs=[hbm] * 4,
            out_specs=pl.BlockSpec(memory_space=pltpu.VMEM),
            scratch_shapes=[
                pltpu.VMEM((6, CH, rows, width), BF16),
                pltpu.VMEM((TAPS + 1, CH, TAPS), F32),
                pltpu.VMEM((CH, SPAN * ROWS, 256), BF16),
                pltpu.VMEM(w_in.shape, BF16),
                pltpu.VMEM(w_out.shape, BF16),
                pltpu.VMEM((CH, ROWS, width), F32),
                pltpu.VMEM((GROUPS, ROWS, GCH, width), BF16),
                pltpu.VMEM((GROUPS, peers, GCH, width), BF16),
                pltpu.VMEM((2, 256, width // 2), BF16),
                pltpu.SemaphoreType.DMA((PARTS, 6)),
                pltpu.SemaphoreType.DMA((PARTS, 6)),
                pltpu.SemaphoreType.DMA((GROUPS, peers)),
                pltpu.SemaphoreType.DMA((GROUPS, peers)),
                pltpu.SemaphoreType.DMA((chans,)),
                pltpu.SemaphoreType.DMA((chans,)),
                pltpu.SemaphoreType.DMA((4,)),
                pltpu.SemaphoreType.REGULAR,
            ],
            compiler_params=pltpu.CompilerParams(
                collective_id=0, has_side_effects=True, vmem_limit_bytes=60 * 2**20
            ),
        )(slide, jnp.transpose(kernel_taps, (1, 0, 2)), w_in, w_out)
        return jnp.transpose(got, (2, 1, 0, 3)).reshape(slide.shape)

    return jax.shard_map(shards, mesh=mesh, in_specs=placed, out_specs=placed[0], check_vma=False)
```

```python
import functools

import jax
import jax.numpy as jnp
from jax import lax
from jax.experimental import pallas as pl
from jax.experimental.pallas import tpu as pltpu
from jax.sharding import PartitionSpec as P

MESH = pl.DeviceIdType.MESH
F32 = jnp.float32
BF16 = jnp.bfloat16

TAPS = 31
STEP = 5
SPAN = 7
CH = 16
ROWS = 8
WIN = 48
PARTS = 4
PCH = CH // PARTS
MERGE = 2


def iota(shape, dim):
    return lax.broadcasted_iota(jnp.int32, shape, dim)


def kernel(
    chips,
    chans,
    slide,
    taps,
    w_in,
    w_out,
    out,
    xbuf,
    tbuf,
    toep,
    win_v,
    wout_v,
    mbuf,
    sbuf,
    rbuf,
    obuf,
    send1,
    recv1,
    send2,
    recv2,
    send3,
    recv3,
    loc,
    back_x,
):
    row = lax.axis_index("row")
    y = lax.axis_index("chan")
    chip = row // 2
    k = row % 2
    m = y * 2 + k
    peers = 2 * chans
    last = chip == chips - 1
    below = (chip + 1) % chips
    above = (chip + chips - 1) % chips

    def signal(sem, r, c):
        pl.semaphore_signal(sem, inc=1, device_id=(r, c), device_id_type=MESH)

    barrier = pltpu.get_barrier_semaphore()
    for tk in range(2):
        signal(barrier, above * 2 + tk, y)

    def row_copy(dq, p, tk):
        core = 1 - k if dq == 0 else tk
        first = core * CH + p * PCH
        return pltpu.make_async_remote_copy(
            src_ref=slide.at[pl.ds(first, PCH)],
            dst_ref=xbuf.at[(1 - dq) * 2 + k, pl.ds(p * PCH, PCH)],
            send_sem=send1.at[p, (1 - dq) * 2 + tk],
            recv_sem=recv1.at[p, (1 - dq) * 2 + k],
            device_id=({1: below, 0: chip, -1: above}[dq] * 2 + core, y),
            device_id_type=MESH,
        )

    def send_rows(dq):
        for p in range(PARTS):
            for tk in range(2 if dq else 1):
                row_copy(dq, p, tk).start()

    @pl.when(last)
    def _():
        pl.semaphore_wait(barrier, 2)
        send_rows(1)

    base = jnp.where(last, above, chip)
    for d in range(1, chans):
        for tk in range(2):
            signal(barrier, base * 2 + tk, (y + d) % chans)

    @pl.when(jnp.logical_not(last))
    def _():
        signal(barrier, chip * 2 + 1 - k, y)

    @pl.when(chip < chips - 2)
    def _():
        for tk in range(2):
            signal(barrier, below * 2 + tk, y)

    taps_copy = pltpu.make_async_copy(
        taps.at[:, pl.ds(pl.multiple_of(k * CH, CH), CH)], tbuf.at[pl.ds(0, TAPS)], loc.at[0]
    )
    own_copy = pltpu.make_async_copy(slide.at[pl.ds(k * CH, CH)], xbuf.at[2 + k], loc.at[1])
    win_copy = pltpu.make_async_copy(w_in, win_v, loc.at[2])
    wout_copy = pltpu.make_async_copy(w_out, wout_v, loc.at[3])
    for copy in (taps_copy, own_copy, win_copy, wout_copy):
        copy.start()

    def prepare():
        taps_copy.wait()
        tbuf[TAPS] = jnp.zeros(tbuf.shape[1:], F32)
        lane = iota((TAPS + 1, 256), 1)
        spread = (lane % WIN == iota((TAPS + 1, 256), 0)) & (lane < STEP * WIN)
        spread = spread.astype(BF16)
        keep = iota((TAPS, 256), 1) // WIN == iota((TAPS, 256), 0) % STEP
        pick = iota((SPAN * ROWS, TAPS), 0) // ROWS == iota((SPAN * ROWS, TAPS), 1) // STEP
        pick = pick.astype(BF16)
        plane = jnp.swapaxes(tbuf[...], 0, 1).astype(BF16)
        for c in range(CH):
            wide = lax.dot_general(plane[c], spread, (((0,), (0,)), ((), ())), preferred_element_type=F32)
            wide = jnp.where(keep, wide, 0.0).astype(BF16)
            base = jnp.dot(pick, wide, preferred_element_type=F32)
            for b in range(SPAN):
                band = pltpu.roll(base[b * ROWS : (b + 1) * ROWS], 1, 1, stride=1, stride_axis=0)
                toep[c, pl.ds(b * ROWS, ROWS), :] = band.astype(BF16)

    @pl.when(jnp.logical_not(last))
    def _():
        prepare()
        from_above = jnp.where(chip == 0, 0, 2)
        from_below = jnp.where(chip == chips - 2, peers, 2)
        pl.semaphore_wait(barrier, peers - 1 + from_above + from_below)
        send_rows(1)

    @pl.when(chip >= chips - 2)
    def _():
        for tk in range(2):
            signal(back_x, below * 2 + tk, y)

    @pl.when(jnp.logical_or(last, chip == 0))
    def _():
        pl.semaphore_wait(back_x, 2)

    send_rows(0)
    send_rows(-1)

    @pl.when(last)
    def _():
        prepare()

    far = sorted(range(1, chans), key=lambda d: -min(d, chans - d))
    own_copy.wait()
    zeros = jnp.zeros((256 - STEP * WIN, 256), BF16)

    def take(slot, p):
        part = xbuf.at[slot, pl.ds(p * PCH, PCH)]
        pltpu.make_async_copy(part, part, recv1.at[p, slot]).wait()

    def across(wave, d):
        t = (y + d) % chans
        return pltpu.make_async_remote_copy(
            src_ref=sbuf.at[wave, t],
            dst_ref=rbuf.at[m],
            send_sem=send2.at[wave, d],
            recv_sem=recv2.at[m],
            device_id=(chip * 2 + wave, t),
            device_id_type=MESH,
        )

    for wave in (1, 0):
        for q in range(0, PARTS, MERGE):
            for p in range(q, q + MERGE):
                if wave == 1:
                    for slot in (4, 5, 3 - k, 1):
                        take(slot, p)
                else:
                    take(0, p)
            for c in range(q * PCH, (q + MERGE) * PCH):
                x = [xbuf[j, c] for j in range(wave, 6)]
                total = x[2].astype(F32)
                if wave == 1:
                    x.append(jnp.zeros_like(x[0]))
                cols = [jnp.concatenate(x, axis=0)]
                for b in range(1, STEP):
                    cols.append(pltpu.roll(cols[0], 256 - b, 1))
                prod = jnp.dot(toep[c], jnp.concatenate(cols + [zeros], axis=0), preferred_element_type=F32)
                for b in range(SPAN):
                    piece = prod[b * ROWS : (b + 1) * ROWS]
                    shift = (TAPS // 2 - STEP * b) % 256
                    total = total + (pltpu.roll(piece, shift, 1) if shift else piece)
                mbuf[wave, c] = total
        sbuf[wave] = jnp.swapaxes(mbuf[wave], 0, 1).astype(BF16)
        for d in far:
            across(wave, d).start()

        @pl.when(k == wave)
        def _():
            rbuf[m] = sbuf[wave, y]

        @pl.when(k != wave)
        def _():
            across(wave, 0).start()

    win_copy.wait()
    wout_copy.wait()
    for d in range(1, peers):
        part = rbuf.at[(m + d) % peers]
        pltpu.make_async_copy(part, part, recv2.at[(m + d) % peers]).wait()
    inner = rbuf[...].reshape(256, 256).astype(F32)
    flat = rbuf[...].reshape(256, 256)
    branch = jnp.zeros((256, 256), F32)
    for f in range(4):
        v = jnp.dot(win_v[pl.ds(f * 256, 256), :], flat, preferred_element_type=F32)
        hidden = (v * (1.0 + lax.erf(v * (0.5**0.5))) * 0.5).astype(BF16)
        branch = branch + jnp.dot(wout_v[:, pl.ds(f * 256, 256)], hidden, preferred_element_type=F32)
    result = (inner + branch.astype(BF16).astype(F32)).astype(BF16)
    obuf[0] = result[:, :128]
    obuf[1] = result[:, 128:]
    depth = 2 * CH

    def send_back(t, slot):
        return pltpu.make_async_remote_copy(
            src_ref=obuf.at[:, pl.ds(pl.multiple_of(t * depth, depth), depth)],
            dst_ref=out.at[:, y],
            send_sem=send3.at[slot],
            recv_sem=recv3.at[y],
            device_id=(row, t),
            device_id_type=MESH,
        )

    pl.when(y > 0)(send_back(0, 0).start)
    for d in far:
        t = (y + d) % chans
        pl.when(t > 0)(send_back(t, d).start)
    out[:, y] = obuf[:, pl.ds(pl.multiple_of(y * depth, depth), depth), :]

    for p in range(PARTS):
        for dq in (1, 0, -1):
            for tk in range(2 if dq else 1):
                row_copy(dq, p, tk).wait_send()
    for wave in (1, 0):
        for d in far:
            across(wave, d).wait_send()
        pl.when(k != wave)(across(wave, 0).wait_send)
    pl.when(y > 0)(send_back(0, 0).wait_send)
    for d in far:
        t = (y + d) % chans
        pl.when(t > 0)(send_back(t, d).wait_send)
    for d in range(1, chans):
        part = out.at[:, (y + d) % chans]
        pltpu.make_async_copy(part, part, recv3.at[(y + d) % chans]).wait()


def solution(mesh):
    chips = mesh.shape["row"] // 2
    chans = mesh.shape["chan"]
    peers = 2 * chans
    placed = (P("chan", "row", None), P("chan", None, None), P(), P())

    def shards(slide, kernel_taps, w_in, w_out):
        depth, rows, width = slide.shape
        hbm = pl.BlockSpec(memory_space=pltpu.HBM)
        got = pl.pallas_call(
            functools.partial(kernel, chips, chans),
            out_shape=jax.ShapeDtypeStruct((2, rows, depth, width // 2), BF16),
            in_specs=[hbm] * 4,
            out_specs=pl.BlockSpec(memory_space=pltpu.VMEM),
            scratch_shapes=[
                pltpu.VMEM((6, CH, rows, width), BF16),
                pltpu.VMEM((TAPS + 1, CH, TAPS), F32),
                pltpu.VMEM((CH, SPAN * ROWS, 256), BF16),
                pltpu.VMEM(w_in.shape, BF16),
                pltpu.VMEM(w_out.shape, BF16),
                pltpu.VMEM((2, CH, ROWS, width), F32),
                pltpu.VMEM((2, ROWS, CH, width), BF16),
                pltpu.VMEM((peers, CH, width), BF16),
                pltpu.VMEM((2, 256, width // 2), BF16),
                pltpu.SemaphoreType.DMA((PARTS, 6)),
                pltpu.SemaphoreType.DMA((PARTS, 6)),
                pltpu.SemaphoreType.DMA((2, chans)),
                pltpu.SemaphoreType.DMA((peers,)),
                pltpu.SemaphoreType.DMA((chans,)),
                pltpu.SemaphoreType.DMA((chans,)),
                pltpu.SemaphoreType.DMA((4,)),
                pltpu.SemaphoreType.REGULAR,
            ],
            compiler_params=pltpu.CompilerParams(
                collective_id=0, has_side_effects=True, vmem_limit_bytes=60 * 2**20
            ),
        )(slide, jnp.transpose(kernel_taps, (1, 0, 2)), w_in, w_out)
        return jnp.transpose(got, (2, 1, 0, 3)).reshape(slide.shape)

    return jax.shard_map(shards, mesh=mesh, in_specs=placed, out_specs=placed[0], check_vma=False)
```

```python
import functools

import jax
import jax.numpy as jnp
from jax import lax
from jax.experimental import pallas as pl
from jax.experimental.pallas import tpu as pltpu
from jax.sharding import PartitionSpec as P

MESH = pl.DeviceIdType.MESH
F32 = jnp.float32
BF16 = jnp.bfloat16

TAPS = 31
STEP = 5
SPAN = 7
CH = 16
ROWS = 8
WIN = 48
PARTS = 2
PCH = CH // PARTS
MERGE = 1


def iota(shape, dim):
    return lax.broadcasted_iota(jnp.int32, shape, dim)


def kernel(
    chips,
    chans,
    slide,
    taps,
    w_in,
    w_out,
    out,
    xbuf,
    tbuf,
    toep,
    win_v,
    wout_v,
    mbuf,
    sbuf,
    rbuf,
    obuf,
    send1,
    recv1,
    send2,
    recv2,
    send3,
    recv3,
    loc,
    back_x,
):
    row = lax.axis_index("row")
    y = lax.axis_index("chan")
    chip = row // 2
    k = row % 2
    m = y * 2 + k
    peers = 2 * chans
    last = chip == chips - 1
    below = (chip + 1) % chips
    above = (chip + chips - 1) % chips

    def signal(sem, r, c):
        pl.semaphore_signal(sem, inc=1, device_id=(r, c), device_id_type=MESH)

    barrier = pltpu.get_barrier_semaphore()
    for tk in range(2):
        signal(barrier, above * 2 + tk, y)

    def row_copy(dq, p, tk):
        core = 1 - k if dq == 0 else tk
        first = core * CH + p * PCH
        return pltpu.make_async_remote_copy(
            src_ref=slide.at[pl.ds(first, PCH)],
            dst_ref=xbuf.at[(1 - dq) * 2 + k, pl.ds(p * PCH, PCH)],
            send_sem=send1.at[p, (1 - dq) * 2 + tk],
            recv_sem=recv1.at[p, (1 - dq) * 2 + k],
            device_id=({1: below, 0: chip, -1: above}[dq] * 2 + core, y),
            device_id_type=MESH,
        )

    def send_rows(dq):
        for p in range(PARTS):
            for tk in range(2 if dq else 1):
                row_copy(dq, p, tk).start()

    @pl.when(last)
    def _():
        pl.semaphore_wait(barrier, 2)
        send_rows(1)

    base = jnp.where(last, above, chip)
    for d in range(1, chans):
        for tk in range(2):
            signal(barrier, base * 2 + tk, (y + d) % chans)

    @pl.when(jnp.logical_not(last))
    def _():
        signal(barrier, chip * 2 + 1 - k, y)

    @pl.when(chip < chips - 2)
    def _():
        for tk in range(2):
            signal(barrier, below * 2 + tk, y)

    taps_copy = pltpu.make_async_copy(
        taps.at[:, pl.ds(pl.multiple_of(k * CH, CH), CH)], tbuf.at[pl.ds(0, TAPS)], loc.at[0]
    )
    own_copy = pltpu.make_async_copy(slide.at[pl.ds(k * CH, CH)], xbuf.at[2 + k], loc.at[1])
    win_copy = pltpu.make_async_copy(w_in, win_v, loc.at[2])
    wout_copy = pltpu.make_async_copy(w_out, wout_v, loc.at[3])
    for copy in (taps_copy, own_copy, win_copy, wout_copy):
        copy.start()

    def prepare():
        taps_copy.wait()
        tbuf[TAPS] = jnp.zeros(tbuf.shape[1:], F32)
        lane = iota((TAPS + 1, 256), 1)
        spread = (lane % WIN == iota((TAPS + 1, 256), 0)) & (lane < STEP * WIN)
        spread = spread.astype(BF16)
        keep = iota((TAPS, 256), 1) // WIN == iota((TAPS, 256), 0) % STEP
        pick = iota((SPAN * ROWS, TAPS), 0) // ROWS == iota((SPAN * ROWS, TAPS), 1) // STEP
        pick = pick.astype(BF16)
        plane = jnp.swapaxes(tbuf[...], 0, 1).astype(BF16)
        for c in range(CH):
            wide = lax.dot_general(plane[c], spread, (((0,), (0,)), ((), ())), preferred_element_type=F32)
            wide = jnp.where(keep, wide, 0.0).astype(BF16)
            base = jnp.dot(pick, wide, preferred_element_type=F32)
            for b in range(SPAN):
                band = pltpu.roll(base[b * ROWS : (b + 1) * ROWS], 1, 1, stride=1, stride_axis=0)
                toep[c, pl.ds(b * ROWS, ROWS), :] = band.astype(BF16)

    @pl.when(jnp.logical_not(last))
    def _():
        prepare()
        from_above = jnp.where(chip == 0, 0, 2)
        from_below = jnp.where(chip == chips - 2, peers, 2)
        pl.semaphore_wait(barrier, peers - 1 + from_above + from_below)
        send_rows(1)

    @pl.when(chip >= chips - 2)
    def _():
        for tk in range(2):
            signal(back_x, below * 2 + tk, y)

    @pl.when(jnp.logical_or(last, chip == 0))
    def _():
        pl.semaphore_wait(back_x, 2)

    send_rows(0)
    send_rows(-1)

    @pl.when(last)
    def _():
        prepare()

    far = sorted(range(1, chans), key=lambda d: -min(d, chans - d))
    own_copy.wait()
    zeros = jnp.zeros((256 - STEP * WIN, 256), BF16)

    def take(slot, p):
        part = xbuf.at[slot, pl.ds(p * PCH, PCH)]
        pltpu.make_async_copy(part, part, recv1.at[p, slot]).wait()

    def across(wave, d):
        t = (y + d) % chans
        return pltpu.make_async_remote_copy(
            src_ref=sbuf.at[wave, t],
            dst_ref=rbuf.at[m],
            send_sem=send2.at[wave, d],
            recv_sem=recv2.at[m],
            device_id=(chip * 2 + wave, t),
            device_id_type=MESH,
        )

    for wave in (1, 0):
        for q in range(0, PARTS, MERGE):
            for p in range(q, q + MERGE):
                if wave == 1:
                    for slot in (4, 5, 3 - k, 1):
                        take(slot, p)
                else:
                    take(0, p)
            for c in range(q * PCH, (q + MERGE) * PCH):
                x = [xbuf[j, c] for j in range(wave, 6)]
                total = x[2].astype(F32)
                if wave == 1:
                    x.append(jnp.zeros_like(x[0]))
                cols = [jnp.concatenate(x, axis=0)]
                for b in range(1, STEP):
                    cols.append(pltpu.roll(cols[0], 256 - b, 1))
                prod = jnp.dot(toep[c], jnp.concatenate(cols + [zeros], axis=0), preferred_element_type=F32)
                for b in range(SPAN):
                    piece = prod[b * ROWS : (b + 1) * ROWS]
                    shift = (TAPS // 2 - STEP * b) % 256
                    total = total + (pltpu.roll(piece, shift, 1) if shift else piece)
                mbuf[wave, c] = total
        sbuf[wave] = jnp.swapaxes(mbuf[wave], 0, 1).astype(BF16)
        for d in far:
            across(wave, d).start()

        @pl.when(k == wave)
        def _():
            rbuf[m] = sbuf[wave, y]

        @pl.when(k != wave)
        def _():
            across(wave, 0).start()

    win_copy.wait()
    wout_copy.wait()
    for d in range(1, peers):
        part = rbuf.at[(m + d) % peers]
        pltpu.make_async_copy(part, part, recv2.at[(m + d) % peers]).wait()
    inner = rbuf[...].reshape(256, 256).astype(F32)
    flat = rbuf[...].reshape(256, 256)
    branch = jnp.zeros((256, 256), F32)
    for f in range(4):
        v = jnp.dot(win_v[pl.ds(f * 256, 256), :], flat, preferred_element_type=F32)
        hidden = (v * (1.0 + lax.erf(v * (0.5**0.5))) * 0.5).astype(BF16)
        branch = branch + jnp.dot(wout_v[:, pl.ds(f * 256, 256)], hidden, preferred_element_type=F32)
    result = (inner + branch.astype(BF16).astype(F32)).astype(BF16)
    obuf[0] = result[:, :128]
    obuf[1] = result[:, 128:]
    depth = 2 * CH

    def send_back(t, slot):
        return pltpu.make_async_remote_copy(
            src_ref=obuf.at[:, pl.ds(pl.multiple_of(t * depth, depth), depth)],
            dst_ref=out.at[:, y],
            send_sem=send3.at[slot],
            recv_sem=recv3.at[y],
            device_id=(row, t),
            device_id_type=MESH,
        )

    pl.when(jnp.logical_and(y > 0, k == 1))(send_back(0, 0).start)
    for d in far:
        t = (y + d) % chans
        pl.when(t > 0)(send_back(t, d).start)
    pl.when(jnp.logical_and(y > 0, k == 0))(send_back(0, 0).start)
    out[:, y] = obuf[:, pl.ds(pl.multiple_of(y * depth, depth), depth), :]

    for p in range(PARTS):
        for dq in (1, 0, -1):
            for tk in range(2 if dq else 1):
                row_copy(dq, p, tk).wait_send()
    for wave in (1, 0):
        for d in far:
            across(wave, d).wait_send()
        pl.when(k != wave)(across(wave, 0).wait_send)
    pl.when(y > 0)(send_back(0, 0).wait_send)
    for d in far:
        t = (y + d) % chans
        pl.when(t > 0)(send_back(t, d).wait_send)
    for d in range(1, chans):
        part = out.at[:, (y + d) % chans]
        pltpu.make_async_copy(part, part, recv3.at[(y + d) % chans]).wait()


def solution(mesh):
    chips = mesh.shape["row"] // 2
    chans = mesh.shape["chan"]
    peers = 2 * chans
    placed = (P("chan", "row", None), P("chan", None, None), P(), P())

    def shards(slide, kernel_taps, w_in, w_out):
        depth, rows, width = slide.shape
        hbm = pl.BlockSpec(memory_space=pltpu.HBM)
        got = pl.pallas_call(
            functools.partial(kernel, chips, chans),
            out_shape=pltpu.VMEM((2, rows, depth, width // 2), BF16),
            in_specs=[hbm] * 4,
            out_specs=pl.BlockSpec(memory_space=pltpu.VMEM),
            scratch_shapes=[
                pltpu.VMEM((6, CH, rows, width), BF16),
                pltpu.VMEM((TAPS + 1, CH, TAPS), F32),
                pltpu.VMEM((CH, SPAN * ROWS, 256), BF16),
                pltpu.VMEM(w_in.shape, BF16),
                pltpu.VMEM(w_out.shape, BF16),
                pltpu.VMEM((2, CH, ROWS, width), F32),
                pltpu.VMEM((2, ROWS, CH, width), BF16),
                pltpu.VMEM((peers, CH, width), BF16),
                pltpu.VMEM((2, 256, width // 2), BF16),
                pltpu.SemaphoreType.DMA((PARTS, 6)),
                pltpu.SemaphoreType.DMA((PARTS, 6)),
                pltpu.SemaphoreType.DMA((2, chans)),
                pltpu.SemaphoreType.DMA((peers,)),
                pltpu.SemaphoreType.DMA((chans,)),
                pltpu.SemaphoreType.DMA((chans,)),
                pltpu.SemaphoreType.DMA((4,)),
                pltpu.SemaphoreType.REGULAR,
            ],
            compiler_params=pltpu.CompilerParams(
                collective_id=0, has_side_effects=True, vmem_limit_bytes=60 * 2**20
            ),
        )(slide, jnp.transpose(kernel_taps, (1, 0, 2)), w_in, w_out)
        return jnp.transpose(got, (2, 1, 0, 3)).reshape(slide.shape)

    return jax.shard_map(shards, mesh=mesh, in_specs=placed, out_specs=placed[0], check_vma=False)
```

```python
import functools

import jax
import jax.numpy as jnp
from jax import lax
from jax.experimental import pallas as pl
from jax.experimental.pallas import tpu as pltpu
from jax.sharding import PartitionSpec as P

MESH = pl.DeviceIdType.MESH
F32 = jnp.float32
BF16 = jnp.bfloat16

TAPS = 31
STEP = 5
SPAN = 7
CH = 16
ROWS = 8
WIN = 48
PARTS = 2
PCH = CH // PARTS
MERGE = 1


def iota(shape, dim):
    return lax.broadcasted_iota(jnp.int32, shape, dim)


def kernel(
    chips,
    chans,
    slide,
    taps,
    w_in,
    w_out,
    out,
    xbuf,
    tbuf,
    toep,
    win_v,
    wout_v,
    mbuf,
    sbuf,
    rbuf,
    obuf,
    send1,
    recv1,
    send2,
    recv2,
    send3,
    recv3,
    loc,
    back_x,
):
    row = lax.axis_index("row")
    y = lax.axis_index("chan")
    chip = row // 2
    k = row % 2
    m = y * 2 + k
    peers = 2 * chans
    last = chip == chips - 1
    below = (chip + 1) % chips
    above = (chip + chips - 1) % chips

    def signal(sem, r, c):
        pl.semaphore_signal(sem, inc=1, device_id=(r, c), device_id_type=MESH)

    barrier = pltpu.get_barrier_semaphore()
    for tk in range(2):
        signal(barrier, above * 2 + tk, y)

    def row_copy(dq, p, tk):
        core = 1 - k if dq == 0 else tk
        first = core * CH + p * PCH
        return pltpu.make_async_remote_copy(
            src_ref=slide.at[pl.ds(first, PCH)],
            dst_ref=xbuf.at[(1 - dq) * 2 + k, pl.ds(p * PCH, PCH)],
            send_sem=send1.at[p, (1 - dq) * 2 + tk],
            recv_sem=recv1.at[p, (1 - dq) * 2 + k],
            device_id=({1: below, 0: chip, -1: above}[dq] * 2 + core, y),
            device_id_type=MESH,
        )

    def send_rows(dq):
        for p in range(PARTS):
            for tk in range(2 if dq else 1):
                row_copy(dq, p, tk).start()

    @pl.when(jnp.logical_and(last, k == 1))
    def _():
        pl.semaphore_wait(barrier, 2)
        send_rows(1)

    base = jnp.where(last, above, chip)
    for d in range(1, chans):
        for tk in range(2):
            signal(barrier, base * 2 + tk, (y + d) % chans)

    @pl.when(jnp.logical_not(last))
    def _():
        signal(barrier, chip * 2 + 1 - k, y)

    @pl.when(chip < chips - 2)
    def _():
        for tk in range(2):
            signal(barrier, below * 2 + tk, y)

    taps_copy = pltpu.make_async_copy(
        taps.at[:, pl.ds(pl.multiple_of(k * CH, CH), CH)], tbuf.at[pl.ds(0, TAPS)], loc.at[0]
    )
    own_copy = pltpu.make_async_copy(slide.at[pl.ds(k * CH, CH)], xbuf.at[2 + k], loc.at[1])
    win_copy = pltpu.make_async_copy(w_in, win_v, loc.at[2])
    wout_copy = pltpu.make_async_copy(w_out, wout_v, loc.at[3])
    for copy in (taps_copy, own_copy, win_copy, wout_copy):
        copy.start()

    @pl.when(jnp.logical_and(last, k == 0))
    def _():
        pl.semaphore_wait(barrier, 2)
        send_rows(1)

    def prepare():
        taps_copy.wait()
        tbuf[TAPS] = jnp.zeros(tbuf.shape[1:], F32)
        lane = iota((TAPS + 1, 256), 1)
        spread = (lane % WIN == iota((TAPS + 1, 256), 0)) & (lane < STEP * WIN)
        spread = spread.astype(BF16)
        keep = iota((TAPS, 256), 1) // WIN == iota((TAPS, 256), 0) % STEP
        pick = iota((SPAN * ROWS, TAPS), 0) // ROWS == iota((SPAN * ROWS, TAPS), 1) // STEP
        pick = pick.astype(BF16)
        plane = jnp.swapaxes(tbuf[...], 0, 1).astype(BF16)
        for c in range(CH):
            wide = lax.dot_general(plane[c], spread, (((0,), (0,)), ((), ())), preferred_element_type=F32)
            wide = jnp.where(keep, wide, 0.0).astype(BF16)
            base = jnp.dot(pick, wide, preferred_element_type=F32)
            for b in range(SPAN):
                band = pltpu.roll(base[b * ROWS : (b + 1) * ROWS], 1, 1, stride=1, stride_axis=0)
                toep[c, pl.ds(b * ROWS, ROWS), :] = band.astype(BF16)

    @pl.when(jnp.logical_not(last))
    def _():
        prepare()
        from_above = jnp.where(chip == 0, 0, 2)
        from_below = jnp.where(chip == chips - 2, peers, 2)
        pl.semaphore_wait(barrier, peers - 1 + from_above + from_below)
        send_rows(1)
        send_rows(0)

    @pl.when(chip >= chips - 2)
    def _():
        for tk in range(2):
            signal(back_x, below * 2 + tk, y)

    @pl.when(jnp.logical_or(last, chip == 0))
    def _():
        pl.semaphore_wait(back_x, 2)

    pl.when(last)(lambda: send_rows(0))
    send_rows(-1)

    @pl.when(last)
    def _():
        prepare()

    far = sorted(range(1, chans), key=lambda d: -min(d, chans - d))
    own_copy.wait()
    zeros = jnp.zeros((256 - STEP * WIN, 256), BF16)

    def take(slot, p):
        part = xbuf.at[slot, pl.ds(p * PCH, PCH)]
        pltpu.make_async_copy(part, part, recv1.at[p, slot]).wait()

    def across(wave, d):
        t = (y + d) % chans
        return pltpu.make_async_remote_copy(
            src_ref=sbuf.at[wave, t],
            dst_ref=rbuf.at[m],
            send_sem=send2.at[wave, d],
            recv_sem=recv2.at[m],
            device_id=(chip * 2 + wave, t),
            device_id_type=MESH,
        )

    for wave in (1, 0):
        for q in range(0, PARTS, MERGE):
            for p in range(q, q + MERGE):
                if wave == 1:
                    for slot in (4, 5, 3 - k, 1):
                        take(slot, p)
                else:
                    take(0, p)
            for c in range(q * PCH, (q + MERGE) * PCH):
                x = [xbuf[j, c] for j in range(wave, 6)]
                total = x[2].astype(F32)
                if wave == 1:
                    x.append(jnp.zeros_like(x[0]))
                cols = [jnp.concatenate(x, axis=0)]
                for b in range(1, STEP):
                    cols.append(pltpu.roll(cols[0], 256 - b, 1))
                prod = jnp.dot(toep[c], jnp.concatenate(cols + [zeros], axis=0), preferred_element_type=F32)
                for b in range(SPAN):
                    piece = prod[b * ROWS : (b + 1) * ROWS]
                    shift = (TAPS // 2 - STEP * b) % 256
                    total = total + (pltpu.roll(piece, shift, 1) if shift else piece)
                mbuf[wave, c] = total
        sbuf[wave] = jnp.swapaxes(mbuf[wave], 0, 1).astype(BF16)
        for d in far:
            across(wave, d).start()

        @pl.when(k == wave)
        def _():
            rbuf[m] = sbuf[wave, y]

        @pl.when(k != wave)
        def _():
            across(wave, 0).start()

    win_copy.wait()
    wout_copy.wait()
    for d in range(1, peers):
        part = rbuf.at[(m + d) % peers]
        pltpu.make_async_copy(part, part, recv2.at[(m + d) % peers]).wait()
    inner = rbuf[...].reshape(256, 256).astype(F32)
    flat = rbuf[...].reshape(256, 256)
    branch = jnp.zeros((256, 256), F32)
    for f in range(4):
        v = jnp.dot(win_v[pl.ds(f * 256, 256), :], flat, preferred_element_type=F32)
        hidden = (v * (1.0 + lax.erf(v * (0.5**0.5))) * 0.5).astype(BF16)
        branch = branch + jnp.dot(wout_v[:, pl.ds(f * 256, 256)], hidden, preferred_element_type=F32)
    result = (inner + branch.astype(BF16).astype(F32)).astype(BF16)
    obuf[0] = result[:, :128]
    obuf[1] = result[:, 128:]
    depth = 2 * CH

    def send_back(t, slot):
        return pltpu.make_async_remote_copy(
            src_ref=obuf.at[:, pl.ds(t * depth, depth)],
            dst_ref=out.at[:, y],
            send_sem=send3.at[slot],
            recv_sem=recv3.at[y],
            device_id=(row, t),
            device_id_type=MESH,
        )

    pl.when(jnp.logical_and(y > 0, k == 1))(send_back(0, 0).start)
    early = sorted(range(1, chans), key=lambda t: min(t, chans - t))
    for t in early:
        pl.when(y != t)(send_back(t, t).start)
    pl.when(jnp.logical_and(y > 0, k == 0))(send_back(0, 0).start)
    out[:, y] = obuf[:, pl.ds(pl.multiple_of(y * depth, depth), depth), :]

    for p in range(PARTS):
        for dq in (1, 0, -1):
            for tk in range(2 if dq else 1):
                row_copy(dq, p, tk).wait_send()
    for wave in (1, 0):
        for d in far:
            across(wave, d).wait_send()
        pl.when(k != wave)(across(wave, 0).wait_send)
    for t in range(chans):
        pl.when(y != t)(send_back(t, t).wait_send)
    for d in range(1, chans):
        part = out.at[:, (y + d) % chans]
        pltpu.make_async_copy(part, part, recv3.at[(y + d) % chans]).wait()


def solution(mesh):
    chips = mesh.shape["row"] // 2
    chans = mesh.shape["chan"]
    peers = 2 * chans
    placed = (P("chan", "row", None), P("chan", None, None), P(), P())

    def shards(slide, kernel_taps, w_in, w_out):
        depth, rows, width = slide.shape
        hbm = pl.BlockSpec(memory_space=pltpu.HBM)
        got = pl.pallas_call(
            functools.partial(kernel, chips, chans),
            out_shape=pltpu.VMEM((2, rows, depth, width // 2), BF16),
            in_specs=[hbm] * 4,
            out_specs=pl.BlockSpec(memory_space=pltpu.VMEM),
            scratch_shapes=[
                pltpu.VMEM((6, CH, rows, width), BF16),
                pltpu.VMEM((TAPS + 1, CH, TAPS), F32),
                pltpu.VMEM((CH, SPAN * ROWS, 256), BF16),
                pltpu.VMEM(w_in.shape, BF16),
                pltpu.VMEM(w_out.shape, BF16),
                pltpu.VMEM((2, CH, ROWS, width), F32),
                pltpu.VMEM((2, ROWS, CH, width), BF16),
                pltpu.VMEM((peers, CH, width), BF16),
                pltpu.VMEM((2, 256, width // 2), BF16),
                pltpu.SemaphoreType.DMA((PARTS, 6)),
                pltpu.SemaphoreType.DMA((PARTS, 6)),
                pltpu.SemaphoreType.DMA((2, chans)),
                pltpu.SemaphoreType.DMA((peers,)),
                pltpu.SemaphoreType.DMA((chans,)),
                pltpu.SemaphoreType.DMA((chans,)),
                pltpu.SemaphoreType.DMA((4,)),
                pltpu.SemaphoreType.REGULAR,
            ],
            compiler_params=pltpu.CompilerParams(
                collective_id=0, has_side_effects=True, vmem_limit_bytes=60 * 2**20
            ),
        )(slide, jnp.transpose(kernel_taps, (1, 0, 2)), w_in, w_out)
        return jnp.transpose(got, (2, 1, 0, 3)).reshape(slide.shape)

    return jax.shard_map(shards, mesh=mesh, in_specs=placed, out_specs=placed[0], check_vma=False)
```

```python
import functools

import jax
import jax.numpy as jnp
from jax import lax
from jax.experimental import pallas as pl
from jax.experimental.pallas import tpu as pltpu
from jax.sharding import PartitionSpec as P

MESH = pl.DeviceIdType.MESH
F32 = jnp.float32
BF16 = jnp.bfloat16

TAPS = 31
STEP = 5
SPAN = 7
CH = 16
ROWS = 8
WIN = 48
PARTS = 2
PCH = CH // PARTS
MERGE = 1


def iota(shape, dim):
    return lax.broadcasted_iota(jnp.int32, shape, dim)


def kernel(
    chips,
    chans,
    slide,
    taps,
    w_in,
    w_out,
    out,
    xbuf,
    tbuf,
    toep,
    win_v,
    wout_v,
    mbuf,
    sbuf,
    rbuf,
    obuf,
    send1,
    recv1,
    send2,
    recv2,
    send3,
    recv3,
    loc,
    back_x,
):
    row = lax.axis_index("row")
    y = lax.axis_index("chan")
    chip = row // 2
    k = row % 2
    m = y * 2 + k
    peers = 2 * chans
    last = chip == chips - 1
    below = (chip + 1) % chips
    above = (chip + chips - 1) % chips

    def signal(sem, r, c):
        pl.semaphore_signal(sem, inc=1, device_id=(r, c), device_id_type=MESH)

    barrier = pltpu.get_barrier_semaphore()
    for tk in range(2):
        signal(barrier, above * 2 + tk, y)

    def row_copy(dq, p, tk):
        core = 1 - k if dq == 0 else tk
        first = core * CH + p * PCH
        return pltpu.make_async_remote_copy(
            src_ref=slide.at[pl.ds(first, PCH)],
            dst_ref=xbuf.at[(1 - dq) * 2 + k, pl.ds(p * PCH, PCH)],
            send_sem=send1.at[p, (1 - dq) * 2 + tk],
            recv_sem=recv1.at[p, (1 - dq) * 2 + k],
            device_id=({1: below, 0: chip, -1: above}[dq] * 2 + core, y),
            device_id_type=MESH,
        )

    def send_rows(dq):
        for p in range(PARTS):
            for tk in range(2 if dq else 1):
                row_copy(dq, p, tk).start()

    @pl.when(jnp.logical_and(last, k == 1))
    def _():
        pl.semaphore_wait(barrier, 2)
        send_rows(1)

    base = jnp.where(last, above, chip)
    for d in range(1, chans):
        for tk in range(2):
            signal(barrier, base * 2 + tk, (y + d) % chans)

    @pl.when(jnp.logical_not(last))
    def _():
        signal(barrier, chip * 2 + 1 - k, y)

    @pl.when(chip < chips - 2)
    def _():
        for tk in range(2):
            signal(barrier, below * 2 + tk, y)

    taps_copy = pltpu.make_async_copy(
        taps.at[:, pl.ds(pl.multiple_of(k * CH, CH), CH)], tbuf.at[pl.ds(0, TAPS)], loc.at[0]
    )
    own_copy = pltpu.make_async_copy(slide.at[pl.ds(k * CH, CH)], xbuf.at[2 + k], loc.at[1])
    win_copy = pltpu.make_async_copy(w_in, win_v, loc.at[2])
    wout_copy = pltpu.make_async_copy(w_out, wout_v, loc.at[3])
    for copy in (taps_copy, own_copy, win_copy, wout_copy):
        copy.start()

    @pl.when(jnp.logical_and(last, k == 0))
    def _():
        pl.semaphore_wait(barrier, 2)
        send_rows(1)

    def prepare():
        taps_copy.wait()
        tbuf[TAPS] = jnp.zeros(tbuf.shape[1:], F32)
        lane = iota((TAPS + 1, 256), 1)
        spread = (lane % WIN == iota((TAPS + 1, 256), 0)) & (lane < STEP * WIN)
        spread = spread.astype(BF16)
        keep = iota((TAPS, 256), 1) // WIN == iota((TAPS, 256), 0) % STEP
        pick = iota((SPAN * ROWS, TAPS), 0) // ROWS == iota((SPAN * ROWS, TAPS), 1) // STEP
        pick = pick.astype(BF16)
        plane = jnp.swapaxes(tbuf[...], 0, 1).astype(BF16)
        for c in range(CH):
            wide = lax.dot_general(plane[c], spread, (((0,), (0,)), ((), ())), preferred_element_type=F32)
            wide = jnp.where(keep, wide, 0.0).astype(BF16)
            base = jnp.dot(pick, wide, preferred_element_type=F32)
            for b in range(SPAN):
                band = pltpu.roll(base[b * ROWS : (b + 1) * ROWS], 1, 1, stride=1, stride_axis=0)
                toep[c, pl.ds(b * ROWS, ROWS), :] = band.astype(BF16)

    @pl.when(jnp.logical_not(last))
    def _():
        prepare()
        from_above = jnp.where(chip == 0, 0, 2)
        from_below = jnp.where(chip == chips - 2, peers, 2)
        pl.semaphore_wait(barrier, peers - 1 + from_above + from_below)
        send_rows(1)
        send_rows(0)

    @pl.when(chip >= chips - 2)
    def _():
        for tk in range(2):
            signal(back_x, below * 2 + tk, y)

    @pl.when(jnp.logical_or(last, chip == 0))
    def _():
        pl.semaphore_wait(back_x, 2)

    pl.when(last)(lambda: send_rows(0))
    send_rows(-1)

    @pl.when(last)
    def _():
        prepare()

    far = sorted(range(1, chans), key=lambda d: -min(d, chans - d))
    own_copy.wait()
    zeros = jnp.zeros((256 - STEP * WIN, 256), BF16)

    def take(slot, p):
        part = xbuf.at[slot, pl.ds(p * PCH, PCH)]
        pltpu.make_async_copy(part, part, recv1.at[p, slot]).wait()

    def across(wave, d):
        t = (y + d) % chans
        return pltpu.make_async_remote_copy(
            src_ref=sbuf.at[wave, t],
            dst_ref=rbuf.at[m],
            send_sem=send2.at[wave, d],
            recv_sem=recv2.at[m],
            device_id=(chip * 2 + wave, t),
            device_id_type=MESH,
        )

    for wave in (1, 0):
        for q in range(0, PARTS, MERGE):
            for p in range(q, q + MERGE):
                if wave == 1:
                    for slot in (4, 5, 3 - k, 1):
                        take(slot, p)
                else:
                    take(0, p)
            for c in range(q * PCH, (q + MERGE) * PCH):
                x = [xbuf[j, c] for j in range(wave, 6)]
                total = x[2].astype(F32)
                if wave == 1:
                    x.append(jnp.zeros_like(x[0]))
                cols = [jnp.concatenate(x, axis=0)]
                for b in range(1, STEP):
                    cols.append(pltpu.roll(cols[0], 256 - b, 1))
                prod = jnp.dot(toep[c], jnp.concatenate(cols + [zeros], axis=0), preferred_element_type=F32)
                for b in range(SPAN):
                    piece = prod[b * ROWS : (b + 1) * ROWS]
                    shift = (TAPS // 2 - STEP * b) % 256
                    total = total + (pltpu.roll(piece, shift, 1) if shift else piece)
                mbuf[wave, c] = total
        sbuf[wave] = jnp.swapaxes(mbuf[wave], 0, 1).astype(BF16)
        for d in far:
            across(wave, d).start()

        @pl.when(k == wave)
        def _():
            rbuf[m] = sbuf[wave, y]

        @pl.when(k != wave)
        def _():
            across(wave, 0).start()

    win_copy.wait()
    wout_copy.wait()
    for d in range(1, peers):
        part = rbuf.at[(m + d) % peers]
        pltpu.make_async_copy(part, part, recv2.at[(m + d) % peers]).wait()
    inner = rbuf[...].reshape(256, 256).astype(F32)
    flat = rbuf[...].reshape(256, 256)
    v = jnp.dot(win_v[...], flat, preferred_element_type=F32)
    hidden = (v * (1.0 + lax.erf(v * (0.5**0.5))) * 0.5).astype(BF16)
    branch = jnp.dot(wout_v[...], hidden, preferred_element_type=F32)
    result = (inner + branch.astype(BF16).astype(F32)).astype(BF16)
    obuf[0] = result[:, :128]
    obuf[1] = result[:, 128:]
    depth = 2 * CH

    def send_back(t, slot):
        return pltpu.make_async_remote_copy(
            src_ref=obuf.at[:, pl.ds(t * depth, depth)],
            dst_ref=out.at[:, y],
            send_sem=send3.at[slot],
            recv_sem=recv3.at[y],
            device_id=(row, t),
            device_id_type=MESH,
        )

    pl.when(jnp.logical_and(y > 0, k == 1))(send_back(0, 0).start)
    early = sorted(range(1, chans), key=lambda t: min(t, chans - t))
    for t in early:
        pl.when(y != t)(send_back(t, t).start)
    pl.when(jnp.logical_and(y > 0, k == 0))(send_back(0, 0).start)
    out[:, y] = obuf[:, pl.ds(pl.multiple_of(y * depth, depth), depth), :]

    for p in range(PARTS):
        for dq in (1, 0, -1):
            for tk in range(2 if dq else 1):
                row_copy(dq, p, tk).wait_send()
    for wave in (1, 0):
        for d in far:
            across(wave, d).wait_send()
        pl.when(k != wave)(across(wave, 0).wait_send)
    for t in range(chans):
        pl.when(y != t)(send_back(t, t).wait_send)
    for d in range(1, chans):
        part = out.at[:, (y + d) % chans]
        pltpu.make_async_copy(part, part, recv3.at[(y + d) % chans]).wait()


def solution(mesh):
    chips = mesh.shape["row"] // 2
    chans = mesh.shape["chan"]
    peers = 2 * chans
    placed = (P("chan", "row", None), P("chan", None, None), P(), P())

    def shards(slide, kernel_taps, w_in, w_out):
        depth, rows, width = slide.shape
        hbm = pl.BlockSpec(memory_space=pltpu.HBM)
        got = pl.pallas_call(
            functools.partial(kernel, chips, chans),
            out_shape=pltpu.VMEM((2, rows, depth, width // 2), BF16),
            in_specs=[hbm] * 4,
            out_specs=pl.BlockSpec(memory_space=pltpu.VMEM),
            scratch_shapes=[
                pltpu.VMEM((6, CH, rows, width), BF16),
                pltpu.VMEM((TAPS + 1, CH, TAPS), F32),
                pltpu.VMEM((CH, SPAN * ROWS, 256), BF16),
                pltpu.VMEM(w_in.shape, BF16),
                pltpu.VMEM(w_out.shape, BF16),
                pltpu.VMEM((2, CH, ROWS, width), F32),
                pltpu.VMEM((2, ROWS, CH, width), BF16),
                pltpu.VMEM((peers, CH, width), BF16),
                pltpu.VMEM((2, 256, width // 2), BF16),
                pltpu.SemaphoreType.DMA((PARTS, 6)),
                pltpu.SemaphoreType.DMA((PARTS, 6)),
                pltpu.SemaphoreType.DMA((2, chans)),
                pltpu.SemaphoreType.DMA((peers,)),
                pltpu.SemaphoreType.DMA((chans,)),
                pltpu.SemaphoreType.DMA((chans,)),
                pltpu.SemaphoreType.DMA((4,)),
                pltpu.SemaphoreType.REGULAR,
            ],
            compiler_params=pltpu.CompilerParams(
                collective_id=0, has_side_effects=True, vmem_limit_bytes=60 * 2**20
            ),
        )(slide, jnp.transpose(kernel_taps, (1, 0, 2)), w_in, w_out)
        return jnp.transpose(got, (2, 1, 0, 3)).reshape(slide.shape)

    return jax.shard_map(shards, mesh=mesh, in_specs=placed, out_specs=placed[0], check_vma=False)
```

```python
import functools

import jax
import jax.numpy as jnp
from jax import lax
from jax.experimental import pallas as pl
from jax.experimental.pallas import tpu as pltpu
from jax.sharding import PartitionSpec as P

MESH = pl.DeviceIdType.MESH
F32 = jnp.float32
BF16 = jnp.bfloat16

TAPS = 31
STEP = 5
SPAN = 7
CH = 16
ROWS = 8
WIN = 48
PARTS = 2
PCH = CH // PARTS
MERGE = 1


def iota(shape, dim):
    return lax.broadcasted_iota(jnp.int32, shape, dim)


def kernel(
    chips,
    chans,
    slide,
    taps,
    w_in,
    w_out,
    final,
    out,
    xbuf,
    tbuf,
    toep,
    win_v,
    wout_v,
    mbuf,
    sbuf,
    rbuf,
    obuf,
    send1,
    recv1,
    send2,
    recv2,
    send3,
    recv3,
    loc,
    back_x,
):
    row = lax.axis_index("row")
    y = lax.axis_index("chan")
    chip = row // 2
    k = row % 2
    m = y * 2 + k
    peers = 2 * chans
    last = chip == chips - 1
    below = (chip + 1) % chips
    above = (chip + chips - 1) % chips

    def signal(sem, r, c):
        pl.semaphore_signal(sem, inc=1, device_id=(r, c), device_id_type=MESH)

    barrier = pltpu.get_barrier_semaphore()
    for tk in range(2):
        signal(barrier, above * 2 + tk, y)

    def row_copy(dq, p, tk):
        core = 1 - k if dq == 0 else tk
        first = core * CH + p * PCH
        return pltpu.make_async_remote_copy(
            src_ref=slide.at[pl.ds(first, PCH)],
            dst_ref=xbuf.at[(1 - dq) * 2 + k, pl.ds(p * PCH, PCH)],
            send_sem=send1.at[p, (1 - dq) * 2 + tk],
            recv_sem=recv1.at[p, (1 - dq) * 2 + k],
            device_id=({1: below, 0: chip, -1: above}[dq] * 2 + core, y),
            device_id_type=MESH,
        )

    def send_rows(dq):
        for p in range(PARTS):
            for tk in range(2 if dq else 1):
                row_copy(dq, p, tk).start()

    @pl.when(jnp.logical_and(last, k == 1))
    def _():
        pl.semaphore_wait(barrier, 2)
        send_rows(1)

    base = jnp.where(last, above, chip)
    for d in range(1, chans):
        for tk in range(2):
            signal(barrier, base * 2 + tk, (y + d) % chans)

    @pl.when(jnp.logical_not(last))
    def _():
        signal(barrier, chip * 2 + 1 - k, y)

    @pl.when(chip < chips - 2)
    def _():
        for tk in range(2):
            signal(barrier, below * 2 + tk, y)

    taps_copy = pltpu.make_async_copy(
        taps.at[:, pl.ds(pl.multiple_of(k * CH, CH), CH)], tbuf.at[pl.ds(0, TAPS)], loc.at[0]
    )
    own_copy = pltpu.make_async_copy(slide.at[pl.ds(k * CH, CH)], xbuf.at[2 + k], loc.at[1])
    win_copy = pltpu.make_async_copy(w_in, win_v, loc.at[2])
    wout_copy = pltpu.make_async_copy(w_out, wout_v, loc.at[3])
    for copy in (taps_copy, own_copy, win_copy, wout_copy):
        copy.start()

    @pl.when(jnp.logical_and(last, k == 0))
    def _():
        pl.semaphore_wait(barrier, 2)
        send_rows(1)

    def prepare():
        taps_copy.wait()
        tbuf[TAPS] = jnp.zeros(tbuf.shape[1:], F32)
        lane = iota((TAPS + 1, 256), 1)
        spread = (lane % WIN == iota((TAPS + 1, 256), 0)) & (lane < STEP * WIN)
        spread = spread.astype(BF16)
        keep = iota((TAPS, 256), 1) // WIN == iota((TAPS, 256), 0) % STEP
        pick = iota((SPAN * ROWS, TAPS), 0) // ROWS == iota((SPAN * ROWS, TAPS), 1) // STEP
        pick = pick.astype(BF16)
        plane = jnp.swapaxes(tbuf[...], 0, 1).astype(BF16)
        for c in range(CH):
            wide = lax.dot_general(plane[c], spread, (((0,), (0,)), ((), ())), preferred_element_type=F32)
            wide = jnp.where(keep, wide, 0.0).astype(BF16)
            base = jnp.dot(pick, wide, preferred_element_type=F32)
            for b in range(SPAN):
                band = pltpu.roll(base[b * ROWS : (b + 1) * ROWS], 1, 1, stride=1, stride_axis=0)
                toep[c, pl.ds(b * ROWS, ROWS), :] = band.astype(BF16)

    @pl.when(jnp.logical_not(last))
    def _():
        prepare()
        from_above = jnp.where(chip == 0, 0, 2)
        from_below = jnp.where(chip == chips - 2, peers, 2)
        pl.semaphore_wait(barrier, peers - 1 + from_above + from_below)
        send_rows(1)
        send_rows(0)

    @pl.when(chip >= chips - 2)
    def _():
        for tk in range(2):
            signal(back_x, below * 2 + tk, y)

    @pl.when(jnp.logical_or(last, chip == 0))
    def _():
        pl.semaphore_wait(back_x, 2)

    pl.when(last)(lambda: send_rows(0))
    send_rows(-1)

    @pl.when(last)
    def _():
        prepare()

    far = sorted(range(1, chans), key=lambda d: -min(d, chans - d))
    own_copy.wait()
    zeros = jnp.zeros((256 - STEP * WIN, 256), BF16)

    def take(slot, p):
        part = xbuf.at[slot, pl.ds(p * PCH, PCH)]
        pltpu.make_async_copy(part, part, recv1.at[p, slot]).wait()

    def across(wave, d):
        t = (y + d) % chans
        return pltpu.make_async_remote_copy(
            src_ref=sbuf.at[wave, t],
            dst_ref=rbuf.at[m],
            send_sem=send2.at[wave, d],
            recv_sem=recv2.at[m],
            device_id=(chip * 2 + wave, t),
            device_id_type=MESH,
        )

    for wave in (1, 0):
        for q in range(0, PARTS, MERGE):
            for p in range(q, q + MERGE):
                if wave == 1:
                    for slot in (4, 5, 3 - k, 1):
                        take(slot, p)
                else:
                    take(0, p)
            for c in range(q * PCH, (q + MERGE) * PCH):
                x = [xbuf[j, c] for j in range(wave, 6)]
                total = x[2].astype(F32)
                if wave == 1:
                    x.append(jnp.zeros_like(x[0]))
                cols = [jnp.concatenate(x, axis=0)]
                for b in range(1, STEP):
                    cols.append(pltpu.roll(cols[0], 256 - b, 1))
                prod = jnp.dot(toep[c], jnp.concatenate(cols + [zeros], axis=0), preferred_element_type=F32)
                for b in range(SPAN):
                    piece = prod[b * ROWS : (b + 1) * ROWS]
                    shift = (TAPS // 2 - STEP * b) % 256
                    total = total + (pltpu.roll(piece, shift, 1) if shift else piece)
                mbuf[wave, c] = total
        sbuf[wave] = jnp.swapaxes(mbuf[wave], 0, 1).astype(BF16)
        for d in far:
            across(wave, d).start()

        @pl.when(k == wave)
        def _():
            rbuf[m] = sbuf[wave, y]

        @pl.when(k != wave)
        def _():
            across(wave, 0).start()

    win_copy.wait()
    wout_copy.wait()
    for d in range(1, peers):
        part = rbuf.at[(m + d) % peers]
        pltpu.make_async_copy(part, part, recv2.at[(m + d) % peers]).wait()
    inner = rbuf[...].reshape(256, 256).astype(F32)
    flat = rbuf[...].reshape(256, 256)
    v = jnp.dot(win_v[...], flat, preferred_element_type=F32)
    hidden = (v * (1.0 + lax.erf(v * (0.5**0.5))) * 0.5).astype(BF16)
    branch = jnp.dot(wout_v[...], hidden, preferred_element_type=F32)
    result = (inner + branch.astype(BF16).astype(F32)).astype(BF16)
    obuf[0] = result[:, :128]
    obuf[1] = result[:, 128:]
    depth = 2 * CH

    def send_back(t, slot):
        return pltpu.make_async_remote_copy(
            src_ref=obuf.at[:, pl.ds(t * depth, depth)],
            dst_ref=out.at[:, y],
            send_sem=send3.at[slot],
            recv_sem=recv3.at[y],
            device_id=(row, t),
            device_id_type=MESH,
        )

    pl.when(jnp.logical_and(y > 0, k == 1))(send_back(0, 0).start)
    early = sorted(range(1, chans), key=lambda t: min(t, chans - t))
    for t in early:
        pl.when(y != t)(send_back(t, t).start)
    pl.when(jnp.logical_and(y > 0, k == 0))(send_back(0, 0).start)
    out[:, y] = obuf[:, pl.ds(pl.multiple_of(y * depth, depth), depth), :]

    for p in range(PARTS):
        for dq in (1, 0, -1):
            for tk in range(2 if dq else 1):
                row_copy(dq, p, tk).wait_send()
    for wave in (1, 0):
        for d in far:
            across(wave, d).wait_send()
        pl.when(k != wave)(across(wave, 0).wait_send)
    for t in range(chans):
        pl.when(y != t)(send_back(t, t).wait_send)
    for d in range(1, chans):
        part = out.at[:, (y + d) % chans]
        pltpu.make_async_copy(part, part, recv3.at[(y + d) % chans]).wait()
    for half in range(2):
        px = pl.ds(half * 128, 128)
        final[:, :, px] = jnp.swapaxes(out[half].astype(F32), 0, 1).astype(BF16)


def solution(mesh):
    chips = mesh.shape["row"] // 2
    chans = mesh.shape["chan"]
    peers = 2 * chans
    placed = (P("chan", "row", None), P("chan", None, None), P(), P())

    def shards(slide, kernel_taps, w_in, w_out):
        depth, rows, width = slide.shape
        hbm = pl.BlockSpec(memory_space=pltpu.HBM)
        got = pl.pallas_call(
            functools.partial(kernel, chips, chans),
            out_shape=pltpu.VMEM((depth, rows, width), BF16),
            in_specs=[hbm] * 4,
            out_specs=pl.BlockSpec(memory_space=pltpu.VMEM),
            scratch_shapes=[
                pltpu.VMEM((2, rows, depth, width // 2), BF16),
                pltpu.VMEM((6, CH, rows, width), BF16),
                pltpu.VMEM((TAPS + 1, CH, TAPS), F32),
                pltpu.VMEM((CH, SPAN * ROWS, 256), BF16),
                pltpu.VMEM(w_in.shape, BF16),
                pltpu.VMEM(w_out.shape, BF16),
                pltpu.VMEM((2, CH, ROWS, width), F32),
                pltpu.VMEM((2, ROWS, CH, width), BF16),
                pltpu.VMEM((peers, CH, width), BF16),
                pltpu.VMEM((2, 256, width // 2), BF16),
                pltpu.SemaphoreType.DMA((PARTS, 6)),
                pltpu.SemaphoreType.DMA((PARTS, 6)),
                pltpu.SemaphoreType.DMA((2, chans)),
                pltpu.SemaphoreType.DMA((peers,)),
                pltpu.SemaphoreType.DMA((chans,)),
                pltpu.SemaphoreType.DMA((chans,)),
                pltpu.SemaphoreType.DMA((4,)),
                pltpu.SemaphoreType.REGULAR,
            ],
            compiler_params=pltpu.CompilerParams(
                collective_id=0, has_side_effects=True, vmem_limit_bytes=60 * 2**20
            ),
        )(slide, jnp.transpose(kernel_taps, (1, 0, 2)), w_in, w_out)
        return got

    return jax.shard_map(shards, mesh=mesh, in_specs=placed, out_specs=placed[0], check_vma=False)
```

```python
import functools

import jax
import jax.numpy as jnp
from jax import lax
from jax.experimental import pallas as pl
from jax.experimental.pallas import tpu as pltpu
from jax.sharding import PartitionSpec as P

MESH = pl.DeviceIdType.MESH
F32 = jnp.float32
BF16 = jnp.bfloat16

TAPS = 31
STEP = 5
SPAN = 7
CH = 16
ROWS = 8
WIN = 48
PARTS = 2
PCH = CH // PARTS
MERGE = 1


def iota(shape, dim):
    return lax.broadcasted_iota(jnp.int32, shape, dim)


def kernel(
    chips,
    chans,
    slide,
    taps,
    w_in,
    w_out,
    out,
    xbuf,
    tbuf,
    toep,
    win_v,
    wout_v,
    mbuf,
    sbuf,
    rbuf,
    obuf,
    send1,
    recv1,
    send2,
    recv2,
    send3,
    recv3,
    loc,
    back_x,
):
    row = lax.axis_index("row")
    y = lax.axis_index("chan")
    chip = row // 2
    k = row % 2
    m = y * 2 + k
    peers = 2 * chans
    last = chip == chips - 1
    below = (chip + 1) % chips
    above = (chip + chips - 1) % chips

    def signal(sem, r, c):
        pl.semaphore_signal(sem, inc=1, device_id=(r, c), device_id_type=MESH)

    barrier = pltpu.get_barrier_semaphore()
    for tk in range(2):
        signal(barrier, above * 2 + tk, y)

    def row_copy(dq, p, tk):
        core = 1 - k if dq == 0 else tk
        first = core * CH + p * PCH
        return pltpu.make_async_remote_copy(
            src_ref=slide.at[pl.ds(first, PCH)],
            dst_ref=xbuf.at[(1 - dq) * 2 + k, pl.ds(p * PCH, PCH)],
            send_sem=send1.at[p, (1 - dq) * 2 + tk],
            recv_sem=recv1.at[p, (1 - dq) * 2 + k],
            device_id=({1: below, 0: chip, -1: above}[dq] * 2 + core, y),
            device_id_type=MESH,
        )

    def send_rows(dq):
        for p in range(PARTS):
            for tk in range(2 if dq else 1):
                row_copy(dq, p, tk).start()

    @pl.when(jnp.logical_and(last, k == 1))
    def _():
        pl.semaphore_wait(barrier, 2)
        send_rows(1)

    base = jnp.where(last, above, chip)
    for d in range(1, chans):
        for tk in range(2):
            signal(barrier, base * 2 + tk, (y + d) % chans)

    @pl.when(jnp.logical_not(last))
    def _():
        signal(barrier, chip * 2 + 1 - k, y)

    @pl.when(chip < chips - 2)
    def _():
        for tk in range(2):
            signal(barrier, below * 2 + tk, y)

    taps_copy = pltpu.make_async_copy(
        taps.at[:, pl.ds(pl.multiple_of(k * CH, CH), CH)], tbuf.at[pl.ds(0, TAPS)], loc.at[0]
    )
    own_copy = pltpu.make_async_copy(slide.at[pl.ds(k * CH, CH)], xbuf.at[2 + k], loc.at[1])
    win_copy = pltpu.make_async_copy(w_in, win_v, loc.at[2])
    wout_copy = pltpu.make_async_copy(w_out, wout_v, loc.at[3])
    for copy in (taps_copy, own_copy, win_copy, wout_copy):
        copy.start()

    @pl.when(jnp.logical_and(last, k == 0))
    def _():
        pl.semaphore_wait(barrier, 2)
        send_rows(1)

    def prepare():
        taps_copy.wait()
        tbuf[TAPS] = jnp.zeros(tbuf.shape[1:], F32)
        lane = iota((TAPS + 1, 256), 1)
        spread = (lane % WIN == iota((TAPS + 1, 256), 0)) & (lane < STEP * WIN)
        spread = spread.astype(BF16)
        keep = iota((TAPS, 256), 1) // WIN == iota((TAPS, 256), 0) % STEP
        pick = iota((SPAN * ROWS, TAPS), 0) // ROWS == iota((SPAN * ROWS, TAPS), 1) // STEP
        pick = pick.astype(BF16)
        plane = jnp.swapaxes(tbuf[...], 0, 1).astype(BF16)
        for c in range(CH):
            wide = lax.dot_general(plane[c], spread, (((0,), (0,)), ((), ())), preferred_element_type=F32)
            wide = jnp.where(keep, wide, 0.0).astype(BF16)
            base = jnp.dot(pick, wide, preferred_element_type=F32)
            for b in range(SPAN):
                band = pltpu.roll(base[b * ROWS : (b + 1) * ROWS], 1, 1, stride=1, stride_axis=0)
                toep[c, pl.ds(b * ROWS, ROWS), :] = band.astype(BF16)

    @pl.when(jnp.logical_not(last))
    def _():
        prepare()
        from_above = jnp.where(chip == 0, 0, 2)
        from_below = jnp.where(chip == chips - 2, peers, 2)
        pl.semaphore_wait(barrier, peers - 1 + from_above + from_below)
        send_rows(1)
        send_rows(0)

    @pl.when(chip >= chips - 2)
    def _():
        for tk in range(2):
            signal(back_x, below * 2 + tk, y)

    @pl.when(jnp.logical_or(last, chip == 0))
    def _():
        pl.semaphore_wait(back_x, 2)

    pl.when(last)(lambda: send_rows(0))
    send_rows(-1)

    @pl.when(last)
    def _():
        prepare()

    far = sorted(range(1, chans), key=lambda d: -min(d, chans - d))
    own_copy.wait()
    zeros = jnp.zeros((256 - STEP * WIN, 256), BF16)

    def take(slot, p):
        part = xbuf.at[slot, pl.ds(p * PCH, PCH)]
        pltpu.make_async_copy(part, part, recv1.at[p, slot]).wait()

    def across(wave, d):
        t = (y + d) % chans
        return pltpu.make_async_remote_copy(
            src_ref=sbuf.at[wave, t],
            dst_ref=rbuf.at[m],
            send_sem=send2.at[wave, d],
            recv_sem=recv2.at[m],
            device_id=(chip * 2 + wave, t),
            device_id_type=MESH,
        )

    for wave in (1, 0):
        for q in range(0, PARTS, MERGE):
            for p in range(q, q + MERGE):
                if wave == 1:
                    for slot in (4, 5, 3 - k, 1):
                        take(slot, p)
                else:
                    take(0, p)
            for c in range(q * PCH, (q + MERGE) * PCH):
                x = [xbuf[j, c] for j in range(wave, 6)]
                total = x[2].astype(F32)
                if wave == 1:
                    x.append(jnp.zeros_like(x[0]))
                cols = [jnp.concatenate(x, axis=0)]
                for b in range(1, STEP):
                    cols.append(pltpu.roll(cols[0], 256 - b, 1))
                prod = jnp.dot(toep[c], jnp.concatenate(cols + [zeros], axis=0), preferred_element_type=F32)
                for b in range(SPAN):
                    piece = prod[b * ROWS : (b + 1) * ROWS]
                    shift = (TAPS // 2 - STEP * b) % 256
                    total = total + (pltpu.roll(piece, shift, 1) if shift else piece)
                mbuf[wave, c] = total
        sbuf[wave] = jnp.swapaxes(mbuf[wave], 0, 1).astype(BF16)
        for odd in range(2):
            for d in far:
                if wave == 0:
                    pl.when((y + d) % 2 == odd)(across(wave, d).start)
                elif odd == 0:
                    across(wave, d).start()

        @pl.when(k == wave)
        def _():
            rbuf[m] = sbuf[wave, y]

        @pl.when(k != wave)
        def _():
            across(wave, 0).start()

    win_copy.wait()
    wout_copy.wait()
    for d in range(1, peers):
        part = rbuf.at[(m + d) % peers]
        pltpu.make_async_copy(part, part, recv2.at[(m + d) % peers]).wait()
    inner = rbuf[...].reshape(256, 256).astype(F32)
    flat = rbuf[...].reshape(256, 256)
    v = jnp.dot(win_v[...], flat, preferred_element_type=F32)
    hidden = (v * (1.0 + lax.erf(v * (0.5**0.5))) * 0.5).astype(BF16)
    branch = jnp.dot(wout_v[...], hidden, preferred_element_type=F32)
    result = (inner + branch.astype(BF16).astype(F32)).astype(BF16)
    obuf[0] = result[:, :128]
    obuf[1] = result[:, 128:]
    depth = 2 * CH

    def send_back(t, slot):
        return pltpu.make_async_remote_copy(
            src_ref=obuf.at[:, pl.ds(t * depth, depth)],
            dst_ref=out.at[:, y],
            send_sem=send3.at[slot],
            recv_sem=recv3.at[y],
            device_id=(row, t),
            device_id_type=MESH,
        )

    pl.when(jnp.logical_and(y > 0, k == 1))(send_back(0, 0).start)
    early = sorted(range(1, chans), key=lambda t: min(t, chans - t))
    for t in early:
        pl.when(y != t)(send_back(t, t).start)
    pl.when(jnp.logical_and(y > 0, k == 0))(send_back(0, 0).start)
    out[:, y] = obuf[:, pl.ds(pl.multiple_of(y * depth, depth), depth), :]

    for p in range(PARTS):
        for dq in (1, 0, -1):
            for tk in range(2 if dq else 1):
                row_copy(dq, p, tk).wait_send()
    for wave in (1, 0):
        for d in far:
            across(wave, d).wait_send()
        pl.when(k != wave)(across(wave, 0).wait_send)
    for t in range(chans):
        pl.when(y != t)(send_back(t, t).wait_send)
    for d in range(1, chans):
        part = out.at[:, (y + d) % chans]
        pltpu.make_async_copy(part, part, recv3.at[(y + d) % chans]).wait()


def solution(mesh):
    chips = mesh.shape["row"] // 2
    chans = mesh.shape["chan"]
    peers = 2 * chans
    placed = (P("chan", "row", None), P("chan", None, None), P(), P())

    def shards(slide, kernel_taps, w_in, w_out):
        depth, rows, width = slide.shape
        hbm = pl.BlockSpec(memory_space=pltpu.HBM)
        got = pl.pallas_call(
            functools.partial(kernel, chips, chans),
            out_shape=pltpu.VMEM((2, rows, depth, width // 2), BF16),
            in_specs=[hbm] * 4,
            out_specs=pl.BlockSpec(memory_space=pltpu.VMEM),
            scratch_shapes=[
                pltpu.VMEM((6, CH, rows, width), BF16),
                pltpu.VMEM((TAPS + 1, CH, TAPS), F32),
                pltpu.VMEM((CH, SPAN * ROWS, 256), BF16),
                pltpu.VMEM(w_in.shape, BF16),
                pltpu.VMEM(w_out.shape, BF16),
                pltpu.VMEM((2, CH, ROWS, width), F32),
                pltpu.VMEM((2, ROWS, CH, width), BF16),
                pltpu.VMEM((peers, CH, width), BF16),
                pltpu.VMEM((2, 256, width // 2), BF16),
                pltpu.SemaphoreType.DMA((PARTS, 6)),
                pltpu.SemaphoreType.DMA((PARTS, 6)),
                pltpu.SemaphoreType.DMA((2, chans)),
                pltpu.SemaphoreType.DMA((peers,)),
                pltpu.SemaphoreType.DMA((chans,)),
                pltpu.SemaphoreType.DMA((chans,)),
                pltpu.SemaphoreType.DMA((4,)),
                pltpu.SemaphoreType.REGULAR,
            ],
            compiler_params=pltpu.CompilerParams(
                collective_id=0, has_side_effects=True, vmem_limit_bytes=60 * 2**20
            ),
        )(slide, jnp.transpose(kernel_taps, (1, 0, 2)), w_in, w_out)
        return jnp.transpose(got, (2, 1, 0, 3)).reshape(slide.shape)

    return jax.shard_map(shards, mesh=mesh, in_specs=placed, out_specs=placed[0], check_vma=False)
```
